128 devices in a mesh: tm: 8 (over z, core), space: 16 (over y, x).
Axes of the slice: x: 4, y: 4, z: 4, core: 2. Of those that a mesh axis runs over, the one named last changes fastest.
Arguments:
- init_field: float32 [2, 128, 1024], P(None, 'space'), may hold values from -3 to 3
- guess: float32 [256, 2, 128, 1024], P('tm', None, 'space'), may hold values from -3 to 3
- slab_blocks: int32 [8], replicated, may hold values from 1 to 4, 16 in all
Outputs:
- updated: float32 [256, 2, 128, 1024], P('tm', None, 'space')
The draws below stay inside these ranges and needn't reach their ends.
Inputs may be any that keep to these rules, and one draw needn't show every extreme that they name: slab_blocks sums to 16; some slab holds exactly 4.
All inputs are finite; a program needn't handle non-finite values.
Results may differ from the reference program's by a relative error of at most 0.000028.
Values sent between devices are 32-bit elements; how exact they have to be, the bound alone decides.
No kernel may reach another device: no remote copies, remote signals or barrier semaphores. Data moves between devices by JAX's collectives and lax.ppermute only.
A program may use at most 128 MiB of HBM per device.

```python
import math
import jax
import jax.numpy as jnp
import numpy as np
from jax import lax

NX = 1024
BMEAN = 2
BMAX = 4
NY = 128
N_TM = 8


def level_of(stream_key, extent, shards, smallest, high):
    loudness = 1.0
    for dim, blocks in shards:
        heights = jax.random.uniform(jax.random.fold_in(jax.random.fold_in(stream_key, 6), dim), (blocks,), jnp.float32, smallest / len(shards), high / len(shards))
        loudness = loudness * jnp.repeat(jnp.exp(heights), extent[dim] // blocks).reshape((-1,) + (1,) * (len(extent) - 1 - dim))
    return loudness


def profile(amount, total, most, slope):
    portions = [(1 << 20) // math.isqrt(rank ** slope) + 1 for rank in range(2, amount + 1)]
    surplus, given = total - most - (amount - 1), [1] * (amount - 1)
    while surplus > 0:
        free = [i for i in range(amount - 1) if given[i] < most]
        pool, left = sum([portions[i] for i in free]), surplus
        for i in free:
            extra = min(most - given[i], max(1, left * portions[i] // pool), surplus)
            given[i] = given[i] + extra
            surplus = surplus - extra
    return np.array([most] + given)


def uneven(stream_key, count, total, bound, slope):
    if count == 2:
        one = jax.random.randint(stream_key, (), max(1, total - bound), min(bound, total - 1) + 1)
        return jnp.stack([one, total - one])
    lengths = jnp.asarray(profile(count, total, bound, slope), jnp.int32)
    pairs = (count - 1) // 2
    source_of, receiver = lengths[1:1 + 2 * pairs:2], lengths[2:2 + 2 * pairs:2]
    room = jnp.minimum(source_of - 1, bound - receiver)
    passed = jax.random.randint(jax.random.fold_in(stream_key, 1), (pairs,), 0, 1 << 20) % (room + 1)
    lengths = lengths.at[1:1 + 2 * pairs:2].set(source_of - passed).at[2:2 + 2 * pairs:2].set(receiver + passed)
    return lengths[jax.random.permutation(jax.random.fold_in(stream_key, 2), count)]


def bell_draw(key, extent, width, bound, pieces=(), dtype=jnp.bfloat16):
    drawn = width * jax.random.normal(key, extent, jnp.float32)
    if pieces:
        drawn = drawn * level_of(key, extent, pieces, -0.22, 0.18)
    return jnp.clip(drawn, -bound, bound).astype(dtype)


def setup_inputs(seed: int = 0) -> dict:
    keys = jax.random.split(jax.random.key(seed), 4)
    return {
        "init_field": bell_draw(keys[0], (2, NY, NX), 0.5, 3.0, ((1, 16),), jnp.float32),
        "guess": bell_draw(keys[1], (8 * BMAX * N_TM, 2, NY, NX), 0.5, 3.0, ((0, 8), (2, 16)), jnp.float32),
        "slab_blocks": uneven(keys[2], N_TM, N_TM * BMEAN, BMAX, 2).astype(jnp.int32),
    }


diffusion_rate = (0.0035, 0.028, 0.224)
advection_rate = (0.003, 0.024, 0.192)


def burgers_step(extended, diffusion, advection):
    centre = extended[:, :, 1:-1]
    above_rows = extended[:, :, 2:]
    below_rows = extended[:, :, :-2]
    eastward = jnp.roll(centre, -1, axis=-1)
    westward = jnp.roll(centre, 1, axis=-1)
    laplace = above_rows + below_rows + eastward + westward - 4.0 * centre
    grad_x = eastward - westward
    grad_y = above_rows - below_rows
    return centre + diffusion * laplace - advection * (centre[:, 0:1] * grad_x + centre[:, 1:2] * grad_y)


def one_step(points, level):
    padded = jnp.pad(points, ((0, 0), (0, 0), (1, 1), (0, 0)))
    return burgers_step(padded, diffusion_rate[level], advection_rate[level])


def shifted(points, initial):
    return jnp.concatenate([initial[None], points[:-1]], 0)


def reference(init_field, guess, slab_blocks):
    blocks = slab_blocks.astype(jnp.int32)
    inclusive = jnp.cumsum(blocks).astype(jnp.int32)
    exclusive = (inclusive - blocks).astype(jnp.int32)
    coarse_ids = jnp.arange(N_TM * BMEAN).astype(jnp.int32)
    owner_slab = jnp.sum((inclusive[None, :] <= coarse_ids[:, None]).astype(jnp.int32), axis=1).astype(jnp.int32)
    padded_block = (owner_slab * BMAX + coarse_ids - exclusive[owner_slab]).astype(jnp.int32)
    fine_rows = (8 * padded_block[:, None] + jnp.arange(8).astype(jnp.int32)[None, :]).reshape(-1).astype(jnp.int32)
    points = guess[fine_rows]
    current = shifted(points, init_field)
    for member in range(7):
        current = one_step(current, 0)
    c_points = one_step(current, 0)
    begin_two = shifted(c_points, init_field)
    current = begin_two
    for member in range(7):
        current = one_step(current, 0)
    residue = one_step(current, 0) - c_points
    forcing_one = residue + c_points - one_step(begin_two, 1)
    coarse_total = N_TM * BMEAN
    level_one = c_points.reshape(coarse_total, 8, 2, NY, NX)
    forcing_grid = forcing_one.reshape(coarse_total, 8, 2, NY, NX)
    current = shifted(level_one[:, 7], init_field)
    for member in range(7):
        current = one_step(current, 1) + forcing_grid[:, member]
    coarse_now = one_step(current, 1) + forcing_grid[:, 7]
    heads = shifted(coarse_now, init_field)
    current = heads
    for member in range(7):
        current = one_step(current, 1) + forcing_grid[:, member]
    remainder = forcing_grid[:, 7] - coarse_now + one_step(current, 1)
    forcing_two = remainder + coarse_now - one_step(heads, 2)

    def coarse_turn(state, pushed):
        following = one_step(state[None], 2)[0] + pushed
        return following, following

    _, solved = lax.scan(coarse_turn, init_field, forcing_two)
    current = shifted(solved, init_field)
    collected = []
    for member in range(7):
        current = one_step(current, 1) + forcing_grid[:, member]
        collected.append(current)
    collected.append(solved)
    final = jnp.stack(collected, 1).reshape(coarse_total * 8, 2, NY, NX)
    return jnp.zeros_like(guess).at[fine_rows].set(final)
```

```python
import jax
import jax.numpy as jnp
from jax import lax
from jax.experimental import pallas as pl
from jax.experimental.pallas import tpu as pltpu
from jax.sharding import PartitionSpec as P

diffusion_rate = (0.0035, 0.028, 0.224)
advection_rate = (0.003, 0.024, 0.192)
F32 = jnp.float32

SNAKE = [4 * (s // 4) + (s % 4 if (s // 4) % 2 == 0 else 3 - s % 4) for s in range(16)]
SMEM = pl.BlockSpec(memory_space=pltpu.SMEM)
VMEM = pl.BlockSpec(memory_space=pltpu.VMEM)
SINGLE = (2, 16, 8, 128)
QUAD = (2, 4, 16, 8, 128)


def shape(*dims):
    return jax.ShapeDtypeStruct(dims, F32)


def whole(kernel, outs, inputs, vregs, scratch=()):
    return pl.pallas_call(
        kernel,
        out_shape=outs,
        in_specs=[SMEM] + [VMEM] * inputs,
        out_specs=jax.tree.map(lambda _: VMEM, outs),
        scratch_shapes=list(scratch),
        compiler_params=pltpu.CompilerParams(vmem_limit_bytes=32 * 1024 * 1024),
        cost_estimate=pl.CostEstimate(flops=11 * 1024 * vregs, bytes_accessed=512 * vregs, transcendentals=0),
        name=kernel.__name__,
    )


def lanes():
    return lax.broadcasted_iota(jnp.int32, (8, 128), 1)


def picked(u, index):
    return jnp.take_along_axis(u, index, axis=1, mode="promise_in_bounds")


def exchanged(tiles, sizes):
    tiles, lane = list(tiles), lanes()
    apart = len(tiles) // 2
    for size in sizes:
        lower = (lane // size) % 2 == 0
        for a in range(len(tiles)):
            if (a // apart) % 2 == 0:
                x, y = tiles[a], tiles[a + apart]
                tiles[a] = jnp.where(lower, x, pltpu.roll(y, size, 1))
                tiles[a + apart] = jnp.where(lower, pltpu.roll(x, 128 - size, 1), y)
        apart //= 2
    return tiles


def quad_order():
    lane = lanes()
    return 4 * (lane % 32) + lane // 32


def single_order():
    lane = lanes()
    return 32 * (lane % 4) + lane // 4


def step(p, q, level):
    d = diffusion_rate[level]
    sub = lax.broadcasted_iota(jnp.int32, (8, 128), 0)
    wp, ep, sq, nq = d + p, d - p, d + q, d - q

    def one(u):
        after_last = jnp.where(sub == 7, 0.0, pltpu.roll(u[0], 7, 0))
        before_first = jnp.where(sub == 0, 0.0, pltpu.roll(u[15], 1, 0))
        north = jnp.concatenate([u[1:], after_last[None]], 0)
        south = jnp.concatenate([before_first[None], u[:-1]], 0)
        east = pltpu.roll(u, 127, 2)
        west = pltpu.roll(u, 1, 2)
        return (1.0 - 4.0 * d) * u + ep * east + wp * west + nq * north + sq * south

    return one(p), one(q)


def quad_step(read, write, level):
    d = diffusion_rate[level]
    sub = lax.broadcasted_iota(jnp.int32, (8, 128), 0)

    def row(k):
        return [[read(c, j, k) for j in range(4)] for c in range(2)]

    first = row(0)
    south = [[jnp.where(sub == 0, 0.0, pltpu.roll(u, 1, 0)) for u in us] for us in row(15)]
    beyond = [[jnp.where(sub == 7, 0.0, pltpu.roll(u, 7, 0)) for u in us] for us in first]
    here = first
    for k in range(16):
        north = row(k + 1) if k < 15 else beyond
        edge_east = [pltpu.roll(us[0], 127, 1) for us in here]
        edge_west = [pltpu.roll(us[3], 1, 1) for us in here]
        for j in range(4):
            p, q = here[0][j], here[1][j]
            wp, ep, sq, nq = d + p, d - p, d + q, d - q
            made = []
            for c in range(2):
                east = here[c][j + 1] if j < 3 else edge_east[c]
                west = here[c][j - 1] if j > 0 else edge_west[c]
                made.append(
                    ((1.0 - 4.0 * d) * here[c][j] + ep * east)
                    + (wp * west + nq * north[c][j])
                    + sq * south[c][j]
                )
            write(j, k, *made)
        south, here = here, north


def reader(ref, *lead):
    return lambda c, j, k: ref[(*lead, c, j, k)]


def writer(ref, *lead):
    def write(j, k, p, q):
        ref[(*lead, 0, j, k)] = p
        ref[(*lead, 1, j, k)] = q

    return write


def adder(ref, g, t):
    def write(j, k, p, q):
        ref[0, j, k] = p + g[t, 0, j, k]
        ref[1, j, k] = q + g[t, 1, j, k]

    return write


def eight_fine_steps(a, b):
    @pl.loop(0, 4)
    def _(_):
        quad_step(reader(a), writer(b), 0)
        quad_step(reader(b), writer(a), 0)


def eight_forced_steps(a, b, g):
    @pl.loop(0, 4)
    def _(n):
        quad_step(reader(a), adder(b, g, 2 * n), 1)
        quad_step(reader(b), adder(a, g, 2 * n + 1), 1)


def vectors():
    return [(c, j, k) for c in range(2) for j in range(4) for k in range(16)]


def tail_kernel(slab_blocks, guess, init, out):
    slab = lax.axis_index("tm")
    last = 8 * slab_blocks[slab] - 1
    out[0] = guess[last - 1]
    out[1] = jnp.where(slab == 7, init[...], guess[last])


def windows_kernel(slab_blocks, guess, before, out):
    lane = lanes()
    column = quad_order()
    even_from, odd_from = (column + 96) % 128, (column + 32) % 128
    even_cut, odd_cut = column < 32, column < 96

    @pl.loop(0, 16)
    def _(n):
        t, c = n // 2, n % 2
        evens, odds = [], []
        for i in range(4):
            rows = guess[jnp.maximum(8 * i + t - 2, 0), c]
            if i == 0:
                rows = jnp.where(t < 2, before[jnp.minimum(t, 1), c], rows)
            rows = advection_rate[0] * rows
            tiles = [rows[:, 128 * n : 128 * n + 128] for n in range(8)]
            a = [picked(u, even_from) for u in tiles]
            b = [picked(u, odd_from) for u in tiles]
            evens.append([jnp.where(even_cut, a[n - 1], a[n]) for n in range(8)])
            odds.append([jnp.where(odd_cut, b[n], b[(n + 1) % 8]) for n in range(8)])
        for n in range(8):
            for s, made in ((2 * n, evens), (2 * n + 1, odds)):
                for j, u in enumerate(exchanged([made[i][n] for i in range(4)], (64, 32))):
                    out[SNAKE[s], t, c, j] = u


def fine_kernel(slab_blocks, points, g, v, last, init, a, b):
    slab = lax.axis_index("tm")
    lane = lanes()
    flat = points.reshape(16 * 8 * 2 * 4 * 8, 128)

    def taken(t, c, j, k):
        return flat[pl.ds((k // 8) * 512 + t * 64 + c * 32 + j * 8 + k % 8, 8, stride=1024), :]

    @pl.loop(0, 8)
    def _(t):
        for c, j, k in vectors():
            a[c, j, k] = taken(t, c, j, k)
        eight_fine_steps(a, b)

        @pl.when(t == 0)
        def _():
            start = (lane < 32) & (slab == 0)
            for c, j, k in vectors():
                a[c, j, k] = jnp.where(start, taken(1, c, j, k), a[c, j, k])
                v[c, j, k] = 8.0 * a[c, j, k]

        quad_step(lambda c, j, k: 8.0 * a[c, j, k], writer(g, t), 1)
        eight_fine_steps(a, b)
        for c, j, k in vectors():
            g[t, c, j, k] = 8.0 * a[c, j, k] - g[t, c, j, k]

    for c in range(2):
        for k in range(16):
            u = 8.0 * taken(1, c, 0, k)
            for j in range(1, 4):
                u = jnp.where(lane // 32 == j, pltpu.roll(8.0 * taken(1, c, j, k), 32 * j, 1), u)
            init[c, k] = u

    eight_forced_steps(v, b, g)
    shift = 128 - 32 * (slab_blocks[slab] - 1)
    for c in range(2):
        for k in range(16):
            u = pltpu.roll(v[c, 0, k], shift % 128, 1)
            for j in range(1, 4):
                u = jnp.where(lane // 32 == j, pltpu.roll(v[c, j, k], (shift + 32 * j) % 128, 1), u)
            last[c, k] = u


def second_pass_kernel(slab_blocks, v, arrived, init, g, big, left, right, a, b, coarse):
    slab = lax.axis_index("tm")
    lane = lanes()
    for c in range(2):
        for k in range(16):
            before = jnp.where(slab == 0, init[c, k], arrived[c, k])
            for j in range(4):
                head = before if j == 0 else pltpu.roll(before, 128 - 32 * j, 1)
                a[c, j, k] = jnp.where(lane < 32, head, pltpu.roll(v[c, j, k], 32, 1))
    quad_step(lambda c, j, k: 8.0 * a[c, j, k], writer(coarse), 2)
    eight_forced_steps(a, b, g)
    order = single_order()
    blocks = slab_blocks[slab]
    for c in range(2):
        for k in range(16):
            made = exchanged([8.0 * a[c, j, k] - coarse[c, j, k] for j in range(4)], (64, 32))
            made = [jnp.where(i < blocks, picked(made[i], order), 0.0) for i in range(4)]
            to_left, to_right = pltpu.roll(made[0], 96, 1), pltpu.roll(made[0], 64, 1)
            for i in range(4):
                big[i, c, k] = made[i]
                if i:
                    to_left = jnp.where(lane // 32 == i, pltpu.roll(made[i], (32 * i + 96) % 128, 1), to_left)
                    to_right = jnp.where(lane // 32 == i, pltpu.roll(made[i], (32 * i + 64) % 128, 1), to_right)
            left[c, k] = to_left
            right[c, k] = to_right


def merge_kernel(
    slab_blocks, mine, mine_left, mine_right, mine_init, other, other_left, other_right, other_init, big, init
):
    lane = lanes()
    order = single_order()
    odd = lax.axis_index("tm") % 2
    for slot, centre, lower, upper in (
        (odd, mine, mine_left, mine_right),
        (1 - odd, other, other_left, other_right),
    ):
        for c in range(2):
            for k in range(16):
                low, high = lower[c, k], upper[c, k]
                for i in range(4):
                    u = jnp.where(lane < 32, pltpu.roll(low, (128 - 32 * i) % 128, 1) if i else low, centre[i, c, k])
                    u = jnp.where(lane >= 96, pltpu.roll(high, 96 - 32 * i, 1) if i < 3 else high, u)
                    big[4 * slot + i, c, k] = u
    for c in range(2):
        for k in range(16):
            init[c, k] = 8.0 * picked(jnp.where(odd == 1, other_init[c, k], mine_init[c, k]), order)


def coarse_steps(p, q, big, first, number):
    def turn(i, s):
        a, b = step(s[0], s[1], 2)
        return a + big[i, 0], b + big[i, 1]

    return lax.fori_loop(first, first + number, turn, (p, q))


def sweep_kernel(slab_blocks, state, big, out):
    even = lax.axis_index("tm") // 2 * 2
    p, q = coarse_steps(state[0], state[1], big, 0, slab_blocks[even])
    p, q = coarse_steps(p, q, big, 4, slab_blocks[even + 1])
    out[0] = p
    out[1] = q


def last_pass_kernel(slab_blocks, state, big, g, out, solved, a, b):
    slab = lax.axis_index("tm")
    odd = slab % 2
    lane = lanes()
    order = quad_order()
    flat = out.reshape(16 * 8 * 4 * 8, 128)
    scale = 1.0 / advection_rate[1]
    first_half = lane % 32 < 16

    def put(t, j, k, p, q):
        u = jnp.where(first_half, pltpu.roll(p, 120, 1), pltpu.roll(q, 8, 1))
        flat[pl.ds((k // 8) * 256 + t * 32 + j * 8 + k % 8, 8, stride=512), :] = scale * u

    p, q = coarse_steps(state[0], state[1], big, 0, odd * slab_blocks[slab - odd])
    for i in range(4):
        solved[i, 0] = p
        solved[i, 1] = q
        p, q = step(p, q, 2)
        p, q = p + big[4 * odd + i, 0], q + big[4 * odd + i, 1]
    solved[4, 0] = p
    solved[4, 1] = q

    for k in range(16):
        heads = [
            exchanged([0.125 * picked(solved[i, c, k], order) for i in range(4)], (64, 32)) for c in range(2)
        ]
        ends = [
            exchanged([0.125 * picked(solved[i + 1, c, k], order) for i in range(4)], (64, 32)) for c in range(2)
        ]
        for j in range(4):
            a[0, j, k] = heads[0][j]
            a[1, j, k] = heads[1][j]
            put(7, j, k, ends[0][j], ends[1][j])

    def forced(ref, t):
        def write(j, k, p, q):
            p, q = p + g[t, 0, j, k], q + g[t, 1, j, k]
            ref[0, j, k] = p
            ref[1, j, k] = q
            put(t, j, k, p, q)

        return write

    @pl.loop(0, 3)
    def _(n):
        quad_step(reader(a), forced(b, 2 * n), 1)
        quad_step(reader(b), forced(a, 2 * n + 1), 1)

    quad_step(reader(a), forced(b, 6), 1)


def strips_kernel(slab_blocks, packed, out):
    lane = lanes()
    blocks = slab_blocks[lax.axis_index("tm")]
    order = lane // 64 * 64 + 16 * (lane % 4) + lane % 64 // 4

    @pl.loop(0, 8)
    def _(t):
        for n in range(8):
            made = exchanged([packed[SNAKE[2 * n + h], t, j] for h in range(2) for j in range(4)], (64, 32, 16))
            for i in range(4):
                for c in range(2):
                    u = jnp.where(i < blocks, picked(made[2 * i + c], order), 0.0)
                    out[8 * i + t, c, :, 128 * n : 128 * n + 128] = u


def body(init_field, guess, slab_blocks):
    ring = [(k, (k + 1) % 8) for k in range(8)]
    cores = [(k, k ^ 1) for k in range(8)]
    up = [(SNAKE[s], SNAKE[(s + 1) % 16]) for s in range(16)]
    down = [(SNAKE[(s + 1) % 16], SNAKE[s]) for s in range(16)]
    quad_scratch = pltpu.VMEM(QUAD, F32)

    with jax.named_scope("column_windows"):
        tail = whole(tail_kernel, shape(2, 2, 8, 1024), 2, 32)(slab_blocks, guess, init_field)
        before = lax.ppermute(tail, "tm", ring)
        pieces = whole(windows_kernel, shape(16, 8, 2, 4, 8, 128), 2, 1024)(slab_blocks, guess, before)
        points = lax.all_to_all(pieces, "space", 0, 0, tiled=True)

    with jax.named_scope("fine_and_first_pass"):
        g, v, last, init1 = whole(
            fine_kernel,
            (shape(8, *QUAD), shape(*QUAD), shape(*SINGLE), shape(*SINGLE)),
            1,
            1024 * 18,
            (quad_scratch, quad_scratch),
        )(slab_blocks, points)
        arrived = lax.ppermute(last, "tm", ring)

    with jax.named_scope("second_pass"):
        big, left, right = whole(
            second_pass_kernel,
            (shape(4, *SINGLE), shape(*SINGLE), shape(*SINGLE)),
            4,
            128 * 10,
            (quad_scratch, quad_scratch, quad_scratch),
        )(slab_blocks, v, arrived, init1, g)

    with jax.named_scope("coarsest_level"):
        upper = lax.ppermute(left, "space", down)
        lower = lax.ppermute(right, "space", up)
        others = [lax.ppermute(x, "tm", cores) for x in (big, lower, upper, init1)]
        full, state = whole(merge_kernel, (shape(8, *SINGLE), shape(*SINGLE)), 8, 512)(
            slab_blocks, big, lower, upper, init1, *others
        )
        plane = lax.axis_index("tm") // 2
        for turn in range(3):
            sent = whole(sweep_kernel, shape(*SINGLE), 2, 32 * 8)(slab_blocks, state, full)
            route = [(2 * turn + core, 2 * turn + 2 + core) for core in range(2)]
            came = lax.ppermute(sent, "tm", route)
            state = jnp.where(plane == turn + 1, came, state)

    with jax.named_scope("last_pass"):
        packed = whole(
            last_pass_kernel,
            shape(16, 8, 4, 8, 128),
            3,
            128 * 10,
            (pltpu.VMEM((5, *SINGLE), F32), quad_scratch, quad_scratch),
        )(slab_blocks, state, full, g)
        packed = lax.all_to_all(packed, "space", 0, 0, tiled=True)
        return whole(strips_kernel, shape(*guess.shape), 1, 512)(slab_blocks, packed)


def solution(mesh):
    placed = (P(None, "space", None), P("tm", None, "space", None), P())
    return jax.shard_map(
        body, mesh=mesh, in_specs=placed, out_specs=P("tm", None, "space", None), check_vma=False
    )
```

```python
import jax
import jax.numpy as jnp
from jax import lax
from jax.experimental import pallas as pl
from jax.experimental.pallas import tpu as pltpu
from jax.sharding import PartitionSpec as P

diffusion_rate = (0.0035, 0.028, 0.224)
advection_rate = (0.003, 0.024, 0.192)
F32 = jnp.float32

SNAKE = [4 * (s // 4) + (s % 4 if (s // 4) % 2 == 0 else 3 - s % 4) for s in range(16)]
SMEM = pl.BlockSpec(memory_space=pltpu.SMEM)
VMEM = pl.BlockSpec(memory_space=pltpu.VMEM)
SINGLE = (2, 16, 8, 128)
QUAD = (2, 4, 16, 8, 128)


def shape(*dims):
    return jax.ShapeDtypeStruct(dims, F32)


def whole(kernel, outs, inputs, microseconds, scratch=(), grid=(), out_specs=None):
    specs = [VMEM] * inputs if isinstance(inputs, int) else [VMEM if x is None else x for x in inputs]
    return pl.pallas_call(
        kernel,
        grid=grid,
        out_shape=outs,
        in_specs=[SMEM] + specs,
        out_specs=out_specs or jax.tree.map(lambda _: VMEM, outs),
        scratch_shapes=list(scratch),
        compiler_params=pltpu.CompilerParams(vmem_limit_bytes=12 * 1024 * 1024),
        cost_estimate=pl.CostEstimate(
            flops=microseconds * 10**9, bytes_accessed=microseconds * 3 * 10**6, transcendentals=0
        ),
        name=kernel.__name__,
    )


def lanes():
    return lax.broadcasted_iota(jnp.int32, (8, 128), 1)


def picked(u, index):
    return jnp.take_along_axis(u, index, axis=1, mode="promise_in_bounds")


def exchanged(tiles, sizes, first=0):
    tiles, lane = list(tiles), (lanes() + 128 - first) % 128
    apart = len(tiles) // 2
    for size in sizes:
        lower = (lane // size) % 2 == 0
        for a in range(len(tiles)):
            if (a // apart) % 2 == 0:
                x, y = tiles[a], tiles[a + apart]
                tiles[a] = jnp.where(lower, x, pltpu.roll(y, size, 1))
                tiles[a + apart] = jnp.where(lower, pltpu.roll(x, 128 - size, 1), y)
        apart //= 2
    return tiles


def quad_order():
    lane = lanes()
    return 4 * (lane % 32) + lane // 32


def single_order():
    lane = lanes()
    return 32 * (lane % 4) + lane // 4


def step(p, q, level):
    d = diffusion_rate[level]
    sub = lax.broadcasted_iota(jnp.int32, (8, 128), 0)
    wp, ep, sq, nq = d + p, d - p, d + q, d - q

    def one(u):
        after_last = jnp.where(sub == 7, 0.0, pltpu.roll(u[0], 7, 0))
        before_first = jnp.where(sub == 0, 0.0, pltpu.roll(u[15], 1, 0))
        north = jnp.concatenate([u[1:], after_last[None]], 0)
        south = jnp.concatenate([before_first[None], u[:-1]], 0)
        east = pltpu.roll(u, 127, 2)
        west = pltpu.roll(u, 1, 2)
        return (1.0 - 4.0 * d) * u + ep * east + wp * west + nq * north + sq * south

    return one(p), one(q)


def quad_step(read, write, level):
    d = diffusion_rate[level]
    sub = lax.broadcasted_iota(jnp.int32, (8, 128), 0)

    def row(k):
        return [[read(c, j, k) for j in range(4)] for c in range(2)]

    first = row(0)
    south = [[jnp.where(sub == 0, 0.0, pltpu.roll(u, 1, 0)) for u in us] for us in row(15)]
    beyond = [[jnp.where(sub == 7, 0.0, pltpu.roll(u, 7, 0)) for u in us] for us in first]
    here = first
    for k in range(16):
        north = row(k + 1) if k < 15 else beyond
        edge_east = [pltpu.roll(us[0], 127, 1) for us in here]
        edge_west = [pltpu.roll(us[3], 1, 1) for us in here]
        for j in range(4):
            p, q = here[0][j], here[1][j]
            wp, ep, sq, nq = d + p, d - p, d + q, d - q
            made = []
            for c in range(2):
                east = here[c][j + 1] if j < 3 else edge_east[c]
                west = here[c][j - 1] if j > 0 else edge_west[c]
                made.append(
                    ((1.0 - 4.0 * d) * here[c][j] + ep * east)
                    + (wp * west + nq * north[c][j])
                    + sq * south[c][j]
                )
            write(j, k, *made)
        south, here = here, north


def reader(ref, *lead):
    return lambda c, j, k: ref[(*lead, c, j, k)]


def writer(ref, *lead):
    def write(j, k, p, q):
        ref[(*lead, 0, j, k)] = p
        ref[(*lead, 1, j, k)] = q

    return write


def adder(ref, g, t):
    def write(j, k, p, q):
        ref[0, j, k] = p + g[t, 0, j, k]
        ref[1, j, k] = q + g[t, 1, j, k]

    return write


def eight_fine_steps(a, b):
    @pl.loop(0, 4)
    def _(_):
        quad_step(reader(a), writer(b), 0)
        quad_step(reader(b), writer(a), 0)


def eight_forced_steps(a, b, g):
    @pl.loop(0, 4)
    def _(n):
        quad_step(reader(a), adder(b, g, 2 * n), 1)
        quad_step(reader(b), adder(a, g, 2 * n + 1), 1)


def rows_loop(body):
    pl.loop(0, 16, unroll=8)(body)


def in_each(body):
    @rows_loop
    def _(k):
        for c in range(2):
            for j in range(4):
                body(c, j, k)


def windows_kernel(nb):
    number = 2 * nb

    def kernel(slab_blocks, guess, init, out, made):
        slab = lax.axis_index("tm")
        blocks = slab_blocks[slab]
        lane = lanes()
        n = pl.program_id(0)
        last_c_point = (slab == 7) & (n == number - 1)
        beyond = (lane >= 96, lane < 32)

        @pl.loop(0, 2)
        def _(c):
            def tile(i, at):
                cols = slice(128 * at, 128 * at + 128)
                u = guess[i % nb, i // nb, 0, c, :, cols]
                if i // nb == 4 // nb - 1:
                    u = jnp.where(last_c_point & (i % nb == blocks - 1), init[c, :, cols], u)
                return u

            for odd in range(2):
                order = (quad_order() + 96 + 64 * odd) % 128
                for i in range(4):
                    for at in range(8):
                        u = jnp.where(beyond[odd], tile(i, (at + 7 + 2 * odd) % 8), tile(i, at))
                        made[odd, i, at] = picked(advection_rate[0] * u, order)
            for odd in range(2):
                for at in range(8):
                    quad = exchanged([made[odd, i, at] for i in range(4)], (64, 32))
                    for j in range(4):
                        out[SNAKE[2 * at + odd], n, c, j] = quad[j]

    kernel.__name__ = "windows_kernel"
    return kernel


def spread_kernel(nb):
    number = 2 * nb

    def kernel(slab_blocks, packed, out):
        @pl.loop(0, 16 * number, unroll=4)
        def _(m):
            source, n = m // number, m % number
            for x in range(packed.shape[2]):
                u = packed[source, n, x]
                for r in range(4 // nb):
                    out[source, n + number * r, x] = pltpu.roll(u, 128 - 32 * nb * r, 1) if r else u

    kernel.__name__ = "spread_kernel"
    return kernel


def pack_kernel(nb):
    number = 2 * nb

    def kernel(slab_blocks, full, out):
        group = (lanes() + 120) % 128 // (32 * nb)

        @pl.loop(0, 16 * number, unroll=4)
        def _(m):
            target, n = m // number, m % number
            for x in range(full.shape[2]):
                u = full[target, n, x]
                for r in range(1, 4 // nb):
                    u = jnp.where(group == r, pltpu.roll(full[target, n + number * r, x], 32 * nb * r, 1), u)
                out[target, n, x] = u

    kernel.__name__ = "pack_kernel"
    return kernel


def taker(points):
    number = points.shape[1]
    flat = points.reshape(16 * number * 64, 128)

    def taken(n, c, j, k):
        first = (k // 8) * number * 64 + n * 64 + c * 32 + j * 8 + k % 8
        return flat[pl.ds(first, 8, stride=number * 128), :]

    return taken


def tail_kernel(slab_blocks, points, out):
    lane = lanes()
    taken = taker(points)
    shift = 128 - 32 * (slab_blocks[lax.axis_index("tm")] - 1)

    @rows_loop
    def _(k):
        for n in range(2):
            for c in range(2):
                u = pltpu.roll(taken(n, c, 0, k), shift % 128, 1)
                for j in range(1, 4):
                    u = jnp.where(lane // 32 == j, pltpu.roll(taken(n, c, j, k), (shift + 32 * j) % 128, 1), u)
                out[n, c, k] = u


def chain(load, a, b, g, t, middle):
    @in_each
    def _(c, j, k):
        a[c, j, k] = load(c, j, k)

    @pl.loop(0, 2)
    def _(half):
        eight_fine_steps(a, b)

        @pl.when(half == 0)
        def _():
            middle()
            quad_step(lambda c, j, k: 8.0 * a[c, j, k], writer(g, t), 1)

    @in_each
    def _(c, j, k):
        g[t, c, j, k] = 8.0 * a[c, j, k] - g[t, c, j, k]


def inner_fine_kernel(slab_blocks, points, g, a, b):
    taken = taker(points)
    chain(lambda c, j, k: taken(0, c, j, k), a, b, g, pl.program_id(0), lambda: None)


def outer_fine_kernel(slab_blocks, points, arrived, inner, g, v, last, init, a, b):
    slab = lax.axis_index("tm")
    lane = lanes()
    taken = taker(points)

    def before(t, c, j, k):
        u = arrived[t, c, k]
        return pltpu.roll(u, 128 - 32 * j, 1) if j else u

    @pl.loop(0, 6)
    def _(t):
        @in_each
        def _(c, j, k):
            g[t + 2, c, j, k] = inner[t, c, j, k]

    def middle(t):
        @pl.when(t == 0)
        def _():
            start = (lane < 32) & (slab == 0)

            @in_each
            def _(c, j, k):
                a[c, j, k] = jnp.where(start, before(1, c, j, k), a[c, j, k])
                v[c, j, k] = 8.0 * a[c, j, k]

    def load(t, c, j, k):
        return jnp.where(lane < 32, before(t, c, j, k), pltpu.roll(taken(t, c, j, k), 32, 1))

    @pl.loop(0, 2)
    def _(t):
        chain(lambda c, j, k: load(t, c, j, k), a, b, g, t, lambda: middle(t))

    eight_forced_steps(v, b, g)
    shift = 128 - 32 * (slab_blocks[slab] - 1)

    @rows_loop
    def _(k):
        for c in range(2):
            x = pltpu.roll(v[c, 0, k], shift % 128, 1)
            for j in range(1, 4):
                x = jnp.where(lane // 32 == j, pltpu.roll(v[c, j, k], (shift + 32 * j) % 128, 1), x)
            init[c, k] = 8.0 * arrived[1, c, k]
            last[c, k] = x


def second_pass_kernel(slab_blocks, v, arrived, init, g, big, left, right, a, b, coarse):
    slab = lax.axis_index("tm")
    lane = lanes()

    @rows_loop
    def _(k):
        for c in range(2):
            before = jnp.where(slab == 0, init[c, k], arrived[c, k])
            for j in range(4):
                head = before if j == 0 else pltpu.roll(before, 128 - 32 * j, 1)
                a[c, j, k] = jnp.where(lane < 32, head, pltpu.roll(v[c, j, k], 32, 1))

    quad_step(lambda c, j, k: 8.0 * a[c, j, k], writer(coarse), 2)
    eight_forced_steps(a, b, g)
    blocks = slab_blocks[slab]
    order = single_order()

    @rows_loop
    def _(k):
        for c in range(2):
            made = [8.0 * a[c, j, k] - coarse[c, j, k] for j in range(4)]
            made = exchanged(made, (64, 32))
            made = [jnp.where(i < blocks, picked(made[i], order), 0.0) for i in range(4)]
            to_left, to_right = pltpu.roll(made[0], 96, 1), pltpu.roll(made[0], 64, 1)
            for i in range(4):
                big[i, c, k] = made[i]
                if i:
                    to_left = jnp.where(lane // 32 == i, pltpu.roll(made[i], (32 * i + 96) % 128, 1), to_left)
                    to_right = jnp.where(lane // 32 == i, pltpu.roll(made[i], (32 * i + 64) % 128, 1), to_right)
            left[c, k] = to_left
            right[c, k] = to_right


def merge_kernel(
    slab_blocks, mine, mine_left, mine_right, mine_init, other, other_left, other_right, other_init, big, init, out
):
    lane = lanes()
    order = single_order()
    slab = lax.axis_index("tm")
    odd = slab % 2

    @rows_loop
    def _(k):
        for slot, centre, lower, upper in (
            (odd, mine, mine_left, mine_right),
            (1 - odd, other, other_left, other_right),
        ):
            for c in range(2):
                low, high = lower[c, k], upper[c, k]
                for i in range(4):
                    u = jnp.where(lane < 32, pltpu.roll(low, 128 - 32 * i, 1) if i else low, centre[i, c, k])
                    u = jnp.where(lane >= 96, pltpu.roll(high, 96 - 32 * i, 1) if i < 3 else high, u)
                    big[4 * slot + i, c, k] = u
        for c in range(2):
            init[c, k] = 8.0 * picked(jnp.where(odd == 1, other_init[c, k], mine_init[c, k]), order)

    sweep_kernel(slab_blocks, init, big, out)


def sweep_kernel(slab_blocks, state, big, out):
    even = lax.axis_index("tm") // 2 * 2
    before = slab_blocks[even]

    def turn(n, s):
        slot = jnp.where(n < before, n, n - before + 4)
        p, q = step(s[0], s[1], 2)
        return p + big[slot, 0], q + big[slot, 1]

    p, q = lax.fori_loop(0, before + slab_blocks[even + 1], turn, (state[0], state[1]))
    out[0] = p
    out[1] = q


def solution_kernel(slab_blocks, state, big, heads, ends, solved):
    slab = lax.axis_index("tm")
    odd = slab % 2
    before = slab_blocks[slab - odd]
    order = quad_order()

    def turn(i, s):
        solved[jnp.maximum(i, 0), 0] = s[0]
        solved[jnp.maximum(i, 0), 1] = s[1]
        slot = jnp.where(i < 0, i + before, 4 * odd + i)
        p, q = step(s[0], s[1], 2)
        return p + big[slot, 0], q + big[slot, 1]

    p, q = lax.fori_loop(-odd * before, 4, turn, (state[0], state[1]))
    solved[4, 0] = p
    solved[4, 1] = q

    @rows_loop
    def _(k):
        for c in range(2):
            made = [picked(0.125 * solved[i, c, k], order) for i in range(5)]
            first, last = exchanged(made[:4], (64, 32)), exchanged(made[1:], (64, 32))
            for j in range(4):
                heads[c, j, k] = first[j]
                ends[c, j, k] = last[j]


def last_pass_kernel(slab_blocks, heads, ends, g, out, a, b):
    lane = lanes()
    flat = out.reshape(16 * 8 * 4 * 8, 128)
    scale = 1.0 / advection_rate[1]
    of_p = (lane % 32 >= 8) & (lane % 32 < 24)

    def put(t, j, k, p, q):
        u = jnp.where(of_p, p, pltpu.roll(q, 16, 1))
        flat[pl.ds((k // 8) * 256 + t * 32 + j * 8 + k % 8, 8, stride=512), :] = scale * u

    def forced(ref, t):
        def write(j, k, p, q):
            p, q = p + g[t, 0, j, k], q + g[t, 1, j, k]
            ref[0, j, k] = p
            ref[1, j, k] = q
            put(t, j, k, p, q)

        return write

    @in_each
    def _(c, j, k):
        a[c, j, k] = heads[c, j, k]

    @pl.loop(0, 4)
    def _(n):
        quad_step(reader(a), forced(b, 2 * n), 1)
        quad_step(reader(b), forced(a, 2 * n + 1), 1)

    @rows_loop
    def _(k):
        for j in range(4):
            put(7, j, k, ends[0, j, k], ends[1, j, k])


def strips_kernel(slab_blocks, packed, out):
    lane = lanes()
    blocks = slab_blocks[lax.axis_index("tm")]
    order = (lane // 64 * 64 + 16 * (lane % 4) + lane % 64 // 4 + 8) % 128
    t = pl.program_id(0)
    for n in range(8):
        made = exchanged([packed[SNAKE[2 * n + h], t, j] for h in range(2) for j in range(4)], (64, 32, 16), 8)
        for i in range(4):
            for c in range(2):
                u = jnp.where(i < blocks, picked(made[2 * i + c], order), 0.0)
                out[i, 0, c, :, 128 * n : 128 * n + 128] = u


def body(init_field, guess, slab_blocks):
    ring = [(k, (k + 1) % 8) for k in range(8)]
    cores = [(k, k ^ 1) for k in range(8)]
    up = [(SNAKE[s], SNAKE[(s + 1) % 16]) for s in range(16)]
    down = [(SNAKE[(s + 1) % 16], SNAKE[s]) for s in range(16)]
    quad_scratch = pltpu.VMEM(QUAD, F32)

    slab = lax.axis_index("tm")
    kind = jnp.sum(jnp.where(jnp.arange(8) == slab, jnp.minimum(slab_blocks, 3) - 1, 0))

    def windows(nb):
        def branch(guess, init_field, slab_blocks):
            number = 2 * nb
            block = pl.BlockSpec((nb, 4 // nb, 1, 2, 8, 1024), lambda n: (0, 0, n, 0, 0, 0))
            pieces = whole(
                windows_kernel(nb), shape(16, number, 2, 4, 8, 128), (block, None), 6, [pltpu.VMEM((2, 4, 8, 8, 128), F32)], (number,)
            )(slab_blocks, guess.reshape(4, 4 // nb, number, 2, 8, 1024), init_field)
            points = lax.all_to_all(pieces, "space", 0, 0, tiled=True).reshape(16, number, 8, 8, 128)
            if nb == 4:
                return points
            return whole(spread_kernel(nb), shape(16, 8, 8, 8, 128), 1, 3)(slab_blocks, points)

        return branch

    def strips(nb):
        def branch(packed, slab_blocks):
            if nb < 4:
                packed = whole(pack_kernel(nb), shape(16, 2 * nb, 4, 8, 128), 1, 3)(slab_blocks, packed)
            packed = lax.all_to_all(packed, "space", 0, 0, tiled=True)
            if nb < 4:
                packed = whole(spread_kernel(nb), shape(16, 8, 4, 8, 128), 1, 3)(slab_blocks, packed)
            return packed

        return branch

    with jax.named_scope("column_windows"):
        points = lax.switch(kind, [windows(1), windows(2), windows(4)], guess, init_field, slab_blocks)
        last_two = pl.BlockSpec((16, 2, 8, 8, 128), lambda i: (0, 3, 0, 0, 0))
        tail = whole(tail_kernel, shape(2, *SINGLE), (last_two,), 2, grid=(1,))(slab_blocks, points)
        before = lax.ppermute(tail, "tm", ring)

    with jax.named_scope("fine_and_first_pass"):
        each = pl.BlockSpec((16, 1, 8, 8, 128), lambda t: (0, t, 0, 0, 0))
        fine = whole(
            inner_fine_kernel, shape(6, *QUAD), (each,), 26, (quad_scratch, quad_scratch), grid=(6,)
        )(slab_blocks, points)
        g, v, last, init1 = whole(
            outer_fine_kernel,
            (shape(8, *QUAD), shape(*QUAD), shape(*SINGLE), shape(*SINGLE)),
            (last_two, None, None),
            12,
            (quad_scratch, quad_scratch),
            grid=(1,),
        )(slab_blocks, points, before, fine)
        arrived = lax.ppermute(last, "tm", ring)

    with jax.named_scope("second_pass"):
        big, left, right = whole(
            second_pass_kernel,
            (shape(4, *SINGLE), shape(*SINGLE), shape(*SINGLE)),
            4,
            4,
            (quad_scratch, quad_scratch, quad_scratch),
        )(slab_blocks, v, arrived, init1, g)

    with jax.named_scope("coarsest_level"):
        upper = lax.ppermute(left, "space", down)
        lower = lax.ppermute(right, "space", up)
        others = [lax.ppermute(x, "tm", cores) for x in (big, lower, upper, init1)]
        full, state, sent = whole(merge_kernel, (shape(8, *SINGLE), shape(*SINGLE), shape(*SINGLE)), 8, 2)(
            slab_blocks, big, lower, upper, init1, *others
        )
        plane = slab // 2
        for turn in range(3):
            if turn:
                sent = whole(sweep_kernel, shape(*SINGLE), 2, 1)(slab_blocks, state, full)
            route = [(2 * turn + core, 2 * turn + 2 + core) for core in range(2)]
            came = lax.ppermute(sent, "tm", route)
            state = jnp.where(plane == turn + 1, came, state)

    with jax.named_scope("last_pass"):
        heads, ends = whole(
            solution_kernel, (shape(*QUAD), shape(*QUAD)), 2, 3, (pltpu.VMEM((5, *SINGLE), F32),)
        )(slab_blocks, state, full)
        packed = whole(last_pass_kernel, shape(16, 8, 4, 8, 128), 3, 6, (quad_scratch, quad_scratch))(
            slab_blocks, heads, ends, g
        )
        packed = lax.switch(kind, [strips(1), strips(2), strips(4)], packed, slab_blocks)
        points = pl.BlockSpec((4, 1, 2, 8, 1024), lambda t: (0, t, 0, 0, 0))
        updated = whole(strips_kernel, shape(4, 8, 2, 8, 1024), 1, 5, grid=(8,), out_specs=points)(slab_blocks, packed)
        return updated.reshape(guess.shape)


def solution(mesh):
    placed = (P(None, "space", None), P("tm", None, "space", None), P())
    return jax.shard_map(
        body, mesh=mesh, in_specs=placed, out_specs=P("tm", None, "space", None), check_vma=False
    )
```

```python
import jax
import jax.numpy as jnp
from jax import lax
from jax.experimental import pallas as pl
from jax.experimental.pallas import tpu as pltpu
from jax.sharding import PartitionSpec as P

diffusion_rate = (0.0035, 0.028, 0.224)
advection_rate = (0.003, 0.024, 0.192)
F32 = jnp.float32

SNAKE = [4 * (s // 4) + (s % 4 if (s // 4) % 2 == 0 else 3 - s % 4) for s in range(16)]
SMEM = pl.BlockSpec(memory_space=pltpu.SMEM)
VMEM = pl.BlockSpec(memory_space=pltpu.VMEM)
SINGLE = (2, 16, 8, 128)
QUAD = (2, 4, 16, 8, 128)


def shape(*dims):
    return jax.ShapeDtypeStruct(dims, F32)


def whole(kernel, outs, inputs, microseconds, scratch=(), grid=()):
    specs = [VMEM] * inputs if isinstance(inputs, int) else [VMEM if x is None else x for x in inputs]
    return pl.pallas_call(
        kernel,
        grid=grid,
        out_shape=outs,
        in_specs=[SMEM] + specs,
        out_specs=jax.tree.map(lambda _: VMEM, outs),
        scratch_shapes=list(scratch),
        compiler_params=pltpu.CompilerParams(vmem_limit_bytes=12 * 1024 * 1024),
        cost_estimate=pl.CostEstimate(
            flops=microseconds * 10**9, bytes_accessed=microseconds * 3 * 10**6, transcendentals=0
        ),
        name=kernel.__name__,
    )


def lanes():
    return lax.broadcasted_iota(jnp.int32, (8, 128), 1)


def picked(u, index):
    return jnp.take_along_axis(u, index, axis=1, mode="promise_in_bounds")


def exchanged(tiles, sizes, first=0):
    tiles, lane = list(tiles), (lanes() + 128 - first) % 128
    apart = len(tiles) // 2
    for size in sizes:
        lower = (lane // size) % 2 == 0
        for a in range(len(tiles)):
            if (a // apart) % 2 == 0:
                x, y = tiles[a], tiles[a + apart]
                tiles[a] = jnp.where(lower, x, pltpu.roll(y, size, 1))
                tiles[a + apart] = jnp.where(lower, pltpu.roll(x, 128 - size, 1), y)
        apart //= 2
    return tiles


def quad_order():
    lane = lanes()
    return 4 * (lane % 32) + lane // 32


def single_order():
    lane = lanes()
    return 32 * (lane % 4) + lane // 4


def step(p, q, level):
    d = diffusion_rate[level]
    sub = lax.broadcasted_iota(jnp.int32, (8, 128), 0)
    wp, ep, sq, nq = d + p, d - p, d + q, d - q

    def one(u):
        after_last = jnp.where(sub == 7, 0.0, pltpu.roll(u[0], 7, 0))
        before_first = jnp.where(sub == 0, 0.0, pltpu.roll(u[15], 1, 0))
        north = jnp.concatenate([u[1:], after_last[None]], 0)
        south = jnp.concatenate([before_first[None], u[:-1]], 0)
        east = pltpu.roll(u, 127, 2)
        west = pltpu.roll(u, 1, 2)
        return (1.0 - 4.0 * d) * u + ep * east + wp * west + nq * north + sq * south

    return one(p), one(q)


def quad_step(read, write, level):
    d = diffusion_rate[level]
    sub = lax.broadcasted_iota(jnp.int32, (8, 128), 0)

    def row(k):
        return [[read(c, j, k) for j in range(4)] for c in range(2)]

    first = row(0)
    south = [[jnp.where(sub == 0, 0.0, pltpu.roll(u, 1, 0)) for u in us] for us in row(15)]
    beyond = [[jnp.where(sub == 7, 0.0, pltpu.roll(u, 7, 0)) for u in us] for us in first]
    here = first
    for k in range(16):
        north = row(k + 1) if k < 15 else beyond
        edge_east = [pltpu.roll(us[0], 127, 1) for us in here]
        edge_west = [pltpu.roll(us[3], 1, 1) for us in here]
        for j in range(4):
            p, q = here[0][j], here[1][j]
            wp, ep, sq, nq = d + p, d - p, d + q, d - q
            made = []
            for c in range(2):
                east = here[c][j + 1] if j < 3 else edge_east[c]
                west = here[c][j - 1] if j > 0 else edge_west[c]
                made.append(
                    ((1.0 - 4.0 * d) * here[c][j] + ep * east)
                    + (wp * west + nq * north[c][j])
                    + sq * south[c][j]
                )
            write(j, k, *made)
        south, here = here, north


def reader(ref, *lead):
    return lambda c, j, k: ref[(*lead, c, j, k)]


def writer(ref, *lead):
    def write(j, k, p, q):
        ref[(*lead, 0, j, k)] = p
        ref[(*lead, 1, j, k)] = q

    return write


def adder(ref, g, t):
    def write(j, k, p, q):
        ref[0, j, k] = p + g[t, 0, j, k]
        ref[1, j, k] = q + g[t, 1, j, k]

    return write


def eight_forced_steps(a, b, g):
    @pl.loop(0, 4)
    def _(n):
        quad_step(reader(a), adder(b, g, 2 * n), 1)
        quad_step(reader(b), adder(a, g, 2 * n + 1), 1)


def rows_loop(body):
    pl.loop(0, 16, unroll=8)(body)


def in_each(body):
    @rows_loop
    def _(k):
        for c in range(2):
            for j in range(4):
                body(c, j, k)


def windows_kernel(nb):
    number = 2 * nb

    def kernel(slab_blocks, guess, *refs):
        *extra, init, out, made = refs
        slab = lax.axis_index("tm")
        blocks = slab_blocks[slab]
        lane = lanes()
        n = pl.program_id(0)
        last_c_point = (slab == 7) & (n == number - 1)
        beyond = (lane >= 96, lane < 32)

        @pl.loop(0, 2)
        def _(c):
            def tile(i, at):
                cols = slice(128 * at, 128 * at + 128)
                if nb == 3:
                    if i < 3:
                        return guess[i, 0, 0, c, :, cols]
                    return jnp.where(last_c_point, init[c, :, cols], extra[0][0, 0, 0, c, :, cols])
                u = guess[i % nb, i // nb, 0, c, :, cols]
                if i // nb == 4 // nb - 1:
                    u = jnp.where(last_c_point & (i % nb == blocks - 1), init[c, :, cols], u)
                return u

            for odd in range(2):
                order = (quad_order() + 96 + 64 * odd) % 128
                for i in range(4):
                    for at in range(8):
                        u = jnp.where(beyond[odd], tile(i, (at + 7 + 2 * odd) % 8), tile(i, at))
                        made[odd, i, at] = picked(advection_rate[0] * u, order)
            for odd in range(2):
                for at in range(8):
                    quad = exchanged([made[odd, i, at] for i in range(4)], (64, 32))
                    for j in range(4):
                        out[SNAKE[2 * at + odd], n, c, j] = quad[j]

    kernel.__name__ = "windows_kernel"
    return kernel


def spread_kernel(nb):
    number = 2 * nb

    def kernel(slab_blocks, packed, out):
        group = lanes() // 32
        if nb == 3:

            @pl.loop(0, 16 * packed.shape[2], unroll=4)
            def _(m):
                source, x = m // packed.shape[2], m % packed.shape[2]
                us = [packed[source, n, x] for n in range(6)]
                for n in range(6):
                    out[source, n, x] = us[n]
                for w in range(2):
                    first, second, third = us[3 * w : 3 * w + 3]
                    u = jnp.where(group == 1, pltpu.roll(second, 64, 1), pltpu.roll(first, 32, 1))
                    out[source, 6 + w, x] = jnp.where(group == 2, pltpu.roll(third, 96, 1), u)

            return

        @pl.loop(0, 16 * number, unroll=4)
        def _(m):
            source, n = m // number, m % number
            for x in range(packed.shape[2]):
                u = packed[source, n, x]
                for r in range(4 // nb):
                    out[source, n + number * r, x] = pltpu.roll(u, 128 - 32 * nb * r, 1) if r else u

    kernel.__name__ = "spread_kernel"
    return kernel


def spread_offset_kernel(nb):
    if nb < 3:
        return spread_kernel(nb)

    def kernel(slab_blocks, packed, out):
        group = (lanes() + 120) % 128 // 32

        @pl.loop(0, 16 * packed.shape[2], unroll=4)
        def _(m):
            source, x = m // packed.shape[2], m % packed.shape[2]
            us = [packed[source, n, x] for n in range(6)]
            for n in range(6):
                out[source, n, x] = us[n]
            for w in range(2):
                first, second, third = us[3 * w : 3 * w + 3]
                u = jnp.where(group == 1, pltpu.roll(second, 64, 1), pltpu.roll(first, 32, 1))
                out[source, 6 + w, x] = jnp.where(group == 2, pltpu.roll(third, 96, 1), u)

    kernel.__name__ = "spread_offset_kernel"
    return kernel


def pack_kernel(nb):
    number = 2 * nb

    def kernel(slab_blocks, full, out):
        group = (lanes() + 120) % 128 // (32 if nb == 3 else 32 * nb)
        if nb == 3:

            @pl.loop(0, 16 * full.shape[2], unroll=4)
            def _(m):
                target, x = m // full.shape[2], m % full.shape[2]
                for n in range(6):
                    u = pltpu.roll(full[target, 6 + n // 3, x], 96 - 32 * (n % 3), 1)
                    out[target, n, x] = jnp.where(group == 3, u, full[target, n, x])

            return

        @pl.loop(0, 16 * number, unroll=4)
        def _(m):
            target, n = m // number, m % number
            for x in range(full.shape[2]):
                u = full[target, n, x]
                for r in range(1, 4 // nb):
                    u = jnp.where(group == r, pltpu.roll(full[target, n + number * r, x], 32 * nb * r, 1), u)
                out[target, n, x] = u

    kernel.__name__ = "pack_kernel"
    return kernel


def taker(points):
    number = points.shape[1]
    flat = points.reshape(16 * number * 64, 128)

    def taken(n, c, j, k):
        first = (k // 8) * number * 64 + n * 64 + c * 32 + j * 8 + k % 8
        return flat[pl.ds(first, 8, stride=number * 128), :]

    return taken


def tail_kernel(slab_blocks, points, out):
    lane = lanes()
    taken = taker(points)
    shift = 128 - 32 * (slab_blocks[lax.axis_index("tm")] - 1)

    @rows_loop
    def _(k):
        for n in range(2):
            for c in range(2):
                u = pltpu.roll(taken(n, c, 0, k), shift % 128, 1)
                for j in range(1, 4):
                    u = jnp.where(lane // 32 == j, pltpu.roll(taken(n, c, j, k), (shift + 32 * j) % 128, 1), u)
                out[n, c, k] = u


def chain(load, a, b, g, t, middle):
    def six_steps(x, y):
        @pl.loop(0, 3)
        def _(_):
            quad_step(reader(x), writer(y), 0)
            quad_step(reader(y), writer(x), 0)

    def finish(j, k, p, q):
        g[t, 0, j, k] = 8.0 * p - g[t, 0, j, k]
        g[t, 1, j, k] = 8.0 * q - g[t, 1, j, k]

    quad_step(load, writer(b), 0)
    six_steps(b, a)
    quad_step(reader(b), writer(a), 0)
    middle()
    quad_step(lambda c, j, k: 8.0 * a[c, j, k], writer(g, t), 1)
    six_steps(a, b)
    quad_step(reader(a), writer(b), 0)
    quad_step(reader(b), finish, 0)


def inner_fine_kernel(slab_blocks, points, g, a, b):
    taken = taker(points)
    chain(lambda c, j, k: taken(0, c, j, k), a, b, g, pl.program_id(0), lambda: None)


def outer_fine_kernel(slab_blocks, points, arrived, inner, g, v, last, init, a, b):
    slab = lax.axis_index("tm")
    lane = lanes()
    taken = taker(points)

    def before(t, c, j, k):
        u = arrived[t, c, k]
        return pltpu.roll(u, 128 - 32 * j, 1) if j else u

    @pl.loop(0, 6)
    def _(t):
        @in_each
        def _(c, j, k):
            g[t + 2, c, j, k] = inner[t, c, j, k]

    def middle(t):
        @pl.when(t == 0)
        def _():
            start = (lane < 32) & (slab == 0)

            @in_each
            def _(c, j, k):
                a[c, j, k] = jnp.where(start, before(1, c, j, k), a[c, j, k])
                v[c, j, k] = 8.0 * a[c, j, k]

    def load(t, c, j, k):
        return jnp.where(lane < 32, before(t, c, j, k), pltpu.roll(taken(t, c, j, k), 32, 1))

    @pl.loop(0, 2)
    def _(t):
        chain(lambda c, j, k: load(t, c, j, k), a, b, g, t, lambda: middle(t))

    eight_forced_steps(v, b, g)
    shift = 128 - 32 * (slab_blocks[slab] - 1)

    @rows_loop
    def _(k):
        for c in range(2):
            x = pltpu.roll(v[c, 0, k], shift % 128, 1)
            for j in range(1, 4):
                x = jnp.where(lane // 32 == j, pltpu.roll(v[c, j, k], (shift + 32 * j) % 128, 1), x)
            init[c, k] = 8.0 * arrived[1, c, k]
            last[c, k] = x


def second_pass_kernel(slab_blocks, v, arrived, init, g, big, left, right, a, b, coarse):
    slab = lax.axis_index("tm")
    lane = lanes()

    @rows_loop
    def _(k):
        for c in range(2):
            before = jnp.where(slab == 0, init[c, k], arrived[c, k])
            for j in range(4):
                head = before if j == 0 else pltpu.roll(before, 128 - 32 * j, 1)
                a[c, j, k] = jnp.where(lane < 32, head, pltpu.roll(v[c, j, k], 32, 1))

    quad_step(lambda c, j, k: 8.0 * a[c, j, k], writer(coarse), 2)
    eight_forced_steps(a, b, g)
    blocks = slab_blocks[slab]
    order = single_order()

    @rows_loop
    def _(k):
        for c in range(2):
            made = [8.0 * a[c, j, k] - coarse[c, j, k] for j in range(4)]
            made = exchanged(made, (64, 32))
            made = [jnp.where(i < blocks, picked(made[i], order), 0.0) for i in range(4)]
            to_left, to_right = pltpu.roll(made[0], 96, 1), pltpu.roll(made[0], 64, 1)
            for i in range(4):
                big[i, c, k] = made[i]
                if i:
                    to_left = jnp.where(lane // 32 == i, pltpu.roll(made[i], (32 * i + 96) % 128, 1), to_left)
                    to_right = jnp.where(lane // 32 == i, pltpu.roll(made[i], (32 * i + 64) % 128, 1), to_right)
            left[c, k] = to_left
            right[c, k] = to_right


def merge_kernel(
    slab_blocks, mine, mine_left, mine_right, mine_init, other, other_left, other_right, other_init, big, init, out
):
    lane = lanes()
    order = single_order()
    slab = lax.axis_index("tm")
    odd = slab % 2

    @rows_loop
    def _(k):
        for slot, centre, lower, upper in (
            (odd, mine, mine_left, mine_right),
            (1 - odd, other, other_left, other_right),
        ):
            for c in range(2):
                low, high = lower[c, k], upper[c, k]
                for i in range(4):
                    u = jnp.where(lane < 32, pltpu.roll(low, 128 - 32 * i, 1) if i else low, centre[i, c, k])
                    u = jnp.where(lane >= 96, pltpu.roll(high, 96 - 32 * i, 1) if i < 3 else high, u)
                    big[4 * slot + i, c, k] = u
        for c in range(2):
            init[c, k] = 8.0 * picked(jnp.where(odd == 1, other_init[c, k], mine_init[c, k]), order)

    sweep_kernel(0)(slab_blocks, init, big, out)


def sweep_kernel(plane):
    def kernel(slab_blocks, state, big, out):
        even = lax.axis_index("tm") // 2 * 2
        before = slab_blocks[even]

        @pl.when(even == 2 * plane)
        def _():
            def turn(n, s):
                slot = jnp.where(n < before, n, n - before + 4)
                p, q = step(s[0], s[1], 2)
                return p + big[slot, 0], q + big[slot, 1]

            p, q = lax.fori_loop(0, before + slab_blocks[even + 1], turn, (state[0], state[1]))
            out[0] = p
            out[1] = q

    kernel.__name__ = "sweep_kernel"
    return kernel


def solution_kernel(slab_blocks, state, big, heads, ends, solved):
    slab = lax.axis_index("tm")
    odd = slab % 2
    before = slab_blocks[slab - odd]
    order = quad_order()

    def turn(i, s):
        solved[jnp.maximum(i, 0), 0] = s[0]
        solved[jnp.maximum(i, 0), 1] = s[1]
        slot = jnp.where(i < 0, i + before, 4 * odd + i)
        p, q = step(s[0], s[1], 2)
        return p + big[slot, 0], q + big[slot, 1]

    p, q = lax.fori_loop(-odd * before, 4, turn, (state[0], state[1]))
    solved[4, 0] = p
    solved[4, 1] = q

    @rows_loop
    def _(k):
        for c in range(2):
            made = [picked(0.125 * solved[i, c, k], order) for i in range(5)]
            first, last = exchanged(made[:4], (64, 32)), exchanged(made[1:], (64, 32))
            for j in range(4):
                heads[c, j, k] = first[j]
                ends[c, j, k] = last[j]


def last_pass_kernel(slab_blocks, heads, ends, g, out, a, b):
    lane = lanes()
    flat = out.reshape(16 * 8 * 4 * 8, 128)
    scale = 1.0 / advection_rate[1]
    of_p = (lane % 32 >= 8) & (lane % 32 < 24)

    def put(t, j, k, p, q):
        u = jnp.where(of_p, p, pltpu.roll(q, 16, 1))
        flat[pl.ds((k // 8) * 256 + t * 32 + j * 8 + k % 8, 8, stride=512), :] = scale * u

    def forced(ref, t):
        def write(j, k, p, q):
            p, q = p + g[t, 0, j, k], q + g[t, 1, j, k]
            ref[0, j, k] = p
            ref[1, j, k] = q
            put(t, j, k, p, q)

        return write

    @in_each
    def _(c, j, k):
        a[c, j, k] = heads[c, j, k]

    @pl.loop(0, 4)
    def _(n):
        quad_step(reader(a), forced(b, 2 * n), 1)
        quad_step(reader(b), forced(a, 2 * n + 1), 1)

    @rows_loop
    def _(k):
        for j in range(4):
            put(7, j, k, ends[0, j, k], ends[1, j, k])


def strips_kernel(slab_blocks, packed, out, made):
    lane = lanes()
    blocks = slab_blocks[lax.axis_index("tm")]
    order = (lane // 64 * 64 + 16 * (lane % 4) + lane % 64 // 4 + 8) % 128

    @pl.loop(0, 8)
    def _(t):
        for n in range(8):
            us = [packed[SNAKE[2 * n + h], t, j] for h in range(2) for j in range(4)]
            for x, u in enumerate(exchanged(us, (64, 32, 16), 8)):
                made[t, n, x] = u

    @pl.loop(0, 8)
    def _(t):
        for n in range(8):
            for i in range(4):
                for c in range(2):
                    u = jnp.where(i < blocks, picked(made[t, n, 2 * i + c], order), 0.0)
                    out[8 * i + t, c, :, 128 * n : 128 * n + 128] = u


def body(init_field, guess, slab_blocks):
    ring = [(k, (k + 1) % 8) for k in range(8)]
    cores = [(k, k ^ 1) for k in range(8)]
    up = [(SNAKE[s], SNAKE[(s + 1) % 16]) for s in range(16)]
    down = [(SNAKE[(s + 1) % 16], SNAKE[s]) for s in range(16)]
    quad_scratch = pltpu.VMEM(QUAD, F32)

    slab = lax.axis_index("tm")
    kind = jnp.sum(jnp.where(jnp.arange(8) == slab, slab_blocks - 1, 0))

    def windows(nb):
        def branch(guess, init_field, slab_blocks):
            number, turns = 2 * nb, 1 if nb == 3 else 4 // nb
            strips = guess.reshape(4, turns, 8 // turns, 2, 8, 1024)
            given = [pl.BlockSpec((nb, turns, 1, 2, 8, 1024), lambda n: (0, 0, n, 0, 0, 0))]
            if nb == 3:
                given.append(pl.BlockSpec((1, 1, 1, 2, 8, 1024), lambda n: (n % 3, 0, 6 + n // 3, 0, 0, 0)))
            pieces = whole(
                windows_kernel(nb),
                shape(16, number, 2, 4, 8, 128),
                (*given, None),
                6,
                [pltpu.VMEM((2, 4, 8, 8, 128), F32)],
                (number,),
            )(slab_blocks, *[strips] * len(given), init_field)
            points = lax.all_to_all(pieces, "space", 0, 0, tiled=True).reshape(16, number, 8, 8, 128)
            if nb == 4:
                return points
            return whole(spread_kernel(nb), shape(16, 8, 8, 8, 128), 1, 3)(slab_blocks, points)

        return branch

    def strips(nb):
        def branch(packed, slab_blocks):
            if nb < 4:
                packed = whole(pack_kernel(nb), shape(16, 2 * nb, 4, 8, 128), 1, 3)(slab_blocks, packed)
            packed = lax.all_to_all(packed, "space", 0, 0, tiled=True)
            if nb < 4:
                packed = whole(spread_offset_kernel(nb), shape(16, 8, 4, 8, 128), 1, 3)(slab_blocks, packed)
            return packed

        return branch

    with jax.named_scope("column_windows"):
        points = lax.switch(kind, [windows(nb) for nb in (1, 2, 3, 4)], guess, init_field, slab_blocks)
        last_two = pl.BlockSpec((16, 2, 8, 8, 128), lambda i: (0, 3, 0, 0, 0))
        tail = whole(tail_kernel, shape(2, *SINGLE), (last_two,), 2, grid=(1,))(slab_blocks, points)
        before = lax.ppermute(tail, "tm", ring)

    with jax.named_scope("fine_and_first_pass"):
        each = pl.BlockSpec((16, 1, 8, 8, 128), lambda t: (0, t, 0, 0, 0))
        fine = whole(
            inner_fine_kernel, shape(6, *QUAD), (each,), 26, (quad_scratch, quad_scratch), grid=(6,)
        )(slab_blocks, points)
        g, v, last, init1 = whole(
            outer_fine_kernel,
            (shape(8, *QUAD), shape(*QUAD), shape(*SINGLE), shape(*SINGLE)),
            (last_two, None, None),
            12,
            (quad_scratch, quad_scratch),
            grid=(1,),
        )(slab_blocks, points, before, fine)
        arrived = lax.ppermute(last, "tm", ring)

    with jax.named_scope("second_pass"):
        big, left, right = whole(
            second_pass_kernel,
            (shape(4, *SINGLE), shape(*SINGLE), shape(*SINGLE)),
            4,
            4,
            (quad_scratch, quad_scratch, quad_scratch),
        )(slab_blocks, v, arrived, init1, g)

    with jax.named_scope("coarsest_level"):
        upper = lax.ppermute(left, "space", down)
        lower = lax.ppermute(right, "space", up)
        others = [lax.ppermute(x, "tm", cores) for x in (big, lower, upper, init1)]
        full, state, sent = whole(merge_kernel, (shape(8, *SINGLE), shape(*SINGLE), shape(*SINGLE)), 8, 2)(
            slab_blocks, big, lower, upper, init1, *others
        )
        plane = slab // 2
        for turn in range(3):
            if turn:
                sent = whole(sweep_kernel(turn), shape(*SINGLE), 2, 1)(slab_blocks, state, full)
            route = [(2 * turn + core, 2 * turn + 2 + core) for core in range(2)]
            came = lax.ppermute(sent, "tm", route)
            state = jnp.where(plane == turn + 1, came, state)

    with jax.named_scope("last_pass"):
        heads, ends = whole(
            solution_kernel, (shape(*QUAD), shape(*QUAD)), 2, 3, (pltpu.VMEM((5, *SINGLE), F32),)
        )(slab_blocks, state, full)
        packed = whole(last_pass_kernel, shape(16, 8, 4, 8, 128), 3, 6, (quad_scratch, quad_scratch))(
            slab_blocks, heads, ends, g
        )
        packed = lax.switch(kind, [strips(nb) for nb in (1, 2, 3, 4)], packed, slab_blocks)
        return whole(strips_kernel, shape(*guess.shape), 1, 5, (pltpu.VMEM((8, 8, 8, 8, 128), F32),))(
            slab_blocks, packed
        )


def solution(mesh):
    placed = (P(None, "space", None), P("tm", None, "space", None), P())
    return jax.shard_map(
        body, mesh=mesh, in_specs=placed, out_specs=P("tm", None, "space", None), check_vma=False
    )
```

```python
import jax
import jax.numpy as jnp
from jax import lax
from jax.experimental import pallas as pl
from jax.experimental.pallas import tpu as pltpu
from jax.sharding import PartitionSpec as P

diffusion_rate = (0.0035, 0.028, 0.224)
advection_rate = (0.003, 0.024, 0.192)
F32 = jnp.float32

SNAKE = [4 * (s // 4) + (s % 4 if (s // 4) % 2 == 0 else 3 - s % 4) for s in range(16)]
SMEM = pl.BlockSpec(memory_space=pltpu.SMEM)
VMEM = pl.BlockSpec(memory_space=pltpu.VMEM)
SINGLE = (2, 16, 8, 128)
QUAD = (2, 4, 16, 8, 128)


def shape(*dims):
    return jax.ShapeDtypeStruct(dims, F32)


def whole(kernel, outs, inputs, microseconds, scratch=(), grid=()):
    specs = [VMEM] * inputs if isinstance(inputs, int) else [VMEM if x is None else x for x in inputs]
    return pl.pallas_call(
        kernel,
        grid=grid,
        out_shape=outs,
        in_specs=[SMEM] + specs,
        out_specs=jax.tree.map(lambda _: VMEM, outs),
        scratch_shapes=list(scratch),
        compiler_params=pltpu.CompilerParams(vmem_limit_bytes=12 * 1024 * 1024),
        cost_estimate=pl.CostEstimate(
            flops=microseconds * 10**9, bytes_accessed=microseconds * 3 * 10**6, transcendentals=0
        ),
        name=kernel.__name__,
    )


def lanes():
    return lax.broadcasted_iota(jnp.int32, (8, 128), 1)


def picked(u, index):
    return jnp.take_along_axis(u, index, axis=1, mode="promise_in_bounds")


def exchanged(tiles, sizes, first=0):
    tiles, lane = list(tiles), (lanes() + 128 - first) % 128
    apart = len(tiles) // 2
    for size in sizes:
        lower = (lane // size) % 2 == 0
        for a in range(len(tiles)):
            if (a // apart) % 2 == 0:
                x, y = tiles[a], tiles[a + apart]
                tiles[a] = jnp.where(lower, x, pltpu.roll(y, size, 1))
                tiles[a + apart] = jnp.where(lower, pltpu.roll(x, 128 - size, 1), y)
        apart //= 2
    return tiles


def quad_order():
    lane = lanes()
    return 4 * (lane % 32) + lane // 32


def single_order():
    lane = lanes()
    return 32 * (lane % 4) + lane // 4


def step(p, q, level):
    d = diffusion_rate[level]
    sub = lax.broadcasted_iota(jnp.int32, (8, 128), 0)
    wp, ep, sq, nq = d + p, d - p, d + q, d - q

    def one(u):
        after_last = jnp.where(sub == 7, 0.0, pltpu.roll(u[0], 7, 0))
        before_first = jnp.where(sub == 0, 0.0, pltpu.roll(u[15], 1, 0))
        north = jnp.concatenate([u[1:], after_last[None]], 0)
        south = jnp.concatenate([before_first[None], u[:-1]], 0)
        east = pltpu.roll(u, 127, 2)
        west = pltpu.roll(u, 1, 2)
        return (1.0 - 4.0 * d) * u + ep * east + wp * west + nq * north + sq * south

    return one(p), one(q)


def quad_step(read, write, level):
    d = diffusion_rate[level]
    sub = lax.broadcasted_iota(jnp.int32, (8, 128), 0)

    def row(k):
        return [[read(c, j, k) for j in range(4)] for c in range(2)]

    first = row(0)
    south = [[jnp.where(sub == 0, 0.0, pltpu.roll(u, 1, 0)) for u in us] for us in row(15)]
    beyond = [[jnp.where(sub == 7, 0.0, pltpu.roll(u, 7, 0)) for u in us] for us in first]
    here = first
    for k in range(16):
        north = row(k + 1) if k < 15 else beyond
        edge_east = [pltpu.roll(us[0], 127, 1) for us in here]
        edge_west = [pltpu.roll(us[3], 1, 1) for us in here]
        for j in range(4):
            p, q = here[0][j], here[1][j]
            wp, ep, sq, nq = d + p, d - p, d + q, d - q
            made = []
            for c in range(2):
                east = here[c][j + 1] if j < 3 else edge_east[c]
                west = here[c][j - 1] if j > 0 else edge_west[c]
                made.append(
                    ((1.0 - 4.0 * d) * here[c][j] + ep * east)
                    + (wp * west + nq * north[c][j])
                    + sq * south[c][j]
                )
            write(j, k, *made)
        south, here = here, north


def reader(ref, *lead):
    return lambda c, j, k: ref[(*lead, c, j, k)]


def writer(ref, *lead):
    def write(j, k, p, q):
        ref[(*lead, 0, j, k)] = p
        ref[(*lead, 1, j, k)] = q

    return write


def adder(ref, g, t):
    def write(j, k, p, q):
        ref[0, j, k] = p + g[t, 0, j, k]
        ref[1, j, k] = q + g[t, 1, j, k]

    return write


def eight_forced_steps(a, b, g):
    @pl.loop(0, 4)
    def _(n):
        quad_step(reader(a), adder(b, g, 2 * n), 1)
        quad_step(reader(b), adder(a, g, 2 * n + 1), 1)


def rows_loop(body):
    pl.loop(0, 16, unroll=8)(body)


def in_each(body):
    @rows_loop
    def _(k):
        for c in range(2):
            for j in range(4):
                body(c, j, k)


def windows_kernel(nb):
    number = 2 * nb

    def kernel(slab_blocks, guess, *refs):
        *extra, init, out, made = refs
        slab = lax.axis_index("tm")
        blocks = slab_blocks[slab]
        lane = lanes()
        n = pl.program_id(0)
        last_c_point = (slab == 7) & (n == number - 1)
        beyond = (lane >= 96, lane < 32)

        @pl.loop(0, 2)
        def _(c):
            def tile(i, at):
                cols = slice(128 * at, 128 * at + 128)
                if nb == 3:
                    if i < 3:
                        return guess[i, 0, 0, c, :, cols]
                    return jnp.where(last_c_point, init[c, :, cols], extra[0][0, 0, 0, c, :, cols])
                u = guess[i % nb, i // nb, 0, c, :, cols]
                if i // nb == 4 // nb - 1:
                    u = jnp.where(last_c_point & (i % nb == blocks - 1), init[c, :, cols], u)
                return u

            for odd in range(2):
                order = (quad_order() + 96 + 64 * odd) % 128
                for i in range(4):
                    for at in range(8):
                        u = jnp.where(beyond[odd], tile(i, (at + 7 + 2 * odd) % 8), tile(i, at))
                        made[odd, i, at] = picked(advection_rate[0] * u, order)
            for odd in range(2):
                for at in range(8):
                    quad = exchanged([made[odd, i, at] for i in range(4)], (64, 32))
                    for j in range(4):
                        out[SNAKE[2 * at + odd], n, c, j] = quad[j]

    kernel.__name__ = "windows_kernel"
    return kernel


def gather_kernel(nb):
    def kernel(slab_blocks, packed, out):
        group = lanes() // 32

        @pl.loop(0, 16 * packed.shape[2], unroll=8)
        def _(m):
            source, x = m // packed.shape[2], m % packed.shape[2]
            us = [packed[source, n, x] for n in range(2 * nb)]
            for n in range(2 * nb):
                out[source, n, x] = us[n]
            for w in range(2):
                if nb == 3:
                    first, second, third = us[3 * w : 3 * w + 3]
                    u = jnp.where(group == 1, pltpu.roll(second, 64, 1), pltpu.roll(first, 32, 1))
                    u = jnp.where(group == 2, pltpu.roll(third, 96, 1), u)
                else:
                    u = pltpu.roll(us[2 * nb - 2 + w], 32 * nb, 1)
                out[source, 6 + w, x] = u

    kernel.__name__ = "gather_kernel"
    return kernel


def spread_kernel(nb):
    number = 2 * nb

    def kernel(slab_blocks, packed, out):
        group = (lanes() + 120) % 128 // 32
        if nb == 3:

            @pl.loop(0, 16 * packed.shape[2], unroll=8)
            def _(m):
                source, x = m // packed.shape[2], m % packed.shape[2]
                us = [packed[source, n, x] for n in range(6)]
                for n in range(6):
                    out[source, n, x] = us[n]
                for w in range(2):
                    first, second, third = us[3 * w : 3 * w + 3]
                    u = jnp.where(group == 1, pltpu.roll(second, 64, 1), pltpu.roll(first, 32, 1))
                    out[source, 6 + w, x] = jnp.where(group == 2, pltpu.roll(third, 96, 1), u)

            return

        @pl.loop(0, 16 * number, unroll=8)
        def _(m):
            source, n = m // number, m % number
            for x in range(packed.shape[2]):
                u = packed[source, n, x]
                for r in range(4 // nb):
                    out[source, n + number * r, x] = pltpu.roll(u, 128 - 32 * nb * r, 1) if r else u

    kernel.__name__ = "spread_kernel"
    return kernel


def pack_kernel(nb):
    number = 2 * nb

    def kernel(slab_blocks, full, out):
        group = (lanes() + 120) % 128 // (32 if nb == 3 else 32 * nb)
        if nb == 3:

            @pl.loop(0, 16 * full.shape[2], unroll=8)
            def _(m):
                target, x = m // full.shape[2], m % full.shape[2]
                for n in range(6):
                    u = pltpu.roll(full[target, 6 + n // 3, x], 96 - 32 * (n % 3), 1)
                    out[target, n, x] = jnp.where(group == 3, u, full[target, n, x])

            return

        @pl.loop(0, 16 * number, unroll=8)
        def _(m):
            target, n = m // number, m % number
            for x in range(full.shape[2]):
                u = full[target, n, x]
                for r in range(1, 4 // nb):
                    u = jnp.where(group == r, pltpu.roll(full[target, n + number * r, x], 32 * nb * r, 1), u)
                out[target, n, x] = u

    kernel.__name__ = "pack_kernel"
    return kernel


def taker(points):
    number = points.shape[1]
    flat = points.reshape(16 * number * 64, 128)

    def taken(n, c, j, k):
        first = (k // 8) * number * 64 + n * 64 + c * 32 + j * 8 + k % 8
        return flat[pl.ds(first, 8, stride=number * 128), :]

    return taken


def tail_kernel(slab_blocks, points, out):
    lane = lanes()
    taken = taker(points)
    shift = 128 - 32 * (slab_blocks[lax.axis_index("tm")] - 1)

    @rows_loop
    def _(k):
        for n in range(2):
            for c in range(2):
                u = pltpu.roll(taken(n, c, 0, k), shift % 128, 1)
                for j in range(1, 4):
                    u = jnp.where(lane // 32 == j, pltpu.roll(taken(n, c, j, k), (shift + 32 * j) % 128, 1), u)
                out[n, c, k] = u


def chain(load, a, b, g, t, middle):
    def six_steps(x, y):
        @pl.loop(0, 3)
        def _(_):
            quad_step(reader(x), writer(y), 0)
            quad_step(reader(y), writer(x), 0)

    def finish(j, k, p, q):
        g[t, 0, j, k] = 8.0 * p - g[t, 0, j, k]
        g[t, 1, j, k] = 8.0 * q - g[t, 1, j, k]

    quad_step(load, writer(b), 0)
    six_steps(b, a)
    quad_step(reader(b), writer(a), 0)
    middle()
    quad_step(lambda c, j, k: 8.0 * a[c, j, k], writer(g, t), 1)
    six_steps(a, b)
    quad_step(reader(a), writer(b), 0)
    quad_step(reader(b), finish, 0)


def inner_fine_kernel(slab_blocks, points, g, a, b):
    taken = taker(points)
    blocks = slab_blocks[lax.axis_index("tm")]
    t = pl.program_id(0)

    @pl.when(t < 2 * blocks)
    def _():
        chain(lambda c, j, k: taken(0, c, j, k), a, b, g, t, lambda: None)

    def spread(target, source, shift):
        @in_each
        def _(c, j, k):
            g[target, c, j, k] = pltpu.roll(g[source, c, j, k], shift, 1)

    @pl.when((t == 5) & (blocks == 2))
    def _():
        @pl.loop(0, 2)
        def _(n):
            spread(n + 4, n, 64)

    @pl.when((t == 5) & (blocks == 1))
    def _():
        @pl.loop(0, 2)
        def _(n):
            spread(n + 4, n, 64)
            spread(n + 2, n, 96)


def outer_fine_kernel(slab_blocks, points, arrived, inner, g, v, last, init, a, b):
    slab = lax.axis_index("tm")
    lane = lanes()
    taken = taker(points)

    def before(t, c, j, k):
        u = arrived[t, c, k]
        return pltpu.roll(u, 128 - 32 * j, 1) if j else u

    @pl.loop(0, 6)
    def _(t):
        @in_each
        def _(c, j, k):
            g[t + 2, c, j, k] = inner[t, c, j, k]

    def middle(t):
        @pl.when(t == 0)
        def _():
            start = (lane < 32) & (slab == 0)

            @in_each
            def _(c, j, k):
                a[c, j, k] = jnp.where(start, before(1, c, j, k), a[c, j, k])
                v[c, j, k] = 8.0 * a[c, j, k]

    def load(t, c, j, k):
        return jnp.where(lane < 32, before(t, c, j, k), pltpu.roll(taken(t, c, j, k), 32, 1))

    few = slab_blocks[slab] <= 2

    @pl.when(few)
    def _():
        @in_each
        def _(c, j, k):
            a[c, j, k] = load(1, c, j, k)

        @in_each
        def _(c, j, k):
            a[c, j, k] = jnp.where(lane < 64, load(0, c, j, k), pltpu.roll(a[c, j, k], 64, 1))

        chain(reader(a), a, b, g, 0, lambda: middle(0))

        @in_each
        def _(c, j, k):
            g[1, c, j, k] = pltpu.roll(g[0, c, j, k], 64, 1)

    @pl.when(jnp.logical_not(few))
    def _():
        @pl.loop(0, 2)
        def _(t):
            @in_each
            def _(c, j, k):
                a[c, j, k] = load(t, c, j, k)

            chain(reader(a), a, b, g, t, lambda: middle(t))

    eight_forced_steps(v, b, g)
    shift = 128 - 32 * (slab_blocks[slab] - 1)

    @rows_loop
    def _(k):
        for c in range(2):
            x = pltpu.roll(v[c, 0, k], shift % 128, 1)
            for j in range(1, 4):
                x = jnp.where(lane // 32 == j, pltpu.roll(v[c, j, k], (shift + 32 * j) % 128, 1), x)
            init[c, k] = 8.0 * arrived[1, c, k]
            last[c, k] = x


def second_pass_kernel(slab_blocks, v, arrived, init, g, big, left, right, a, b, coarse):
    slab = lax.axis_index("tm")
    lane = lanes()

    @rows_loop
    def _(k):
        for c in range(2):
            before = jnp.where(slab == 0, init[c, k], arrived[c, k])
            for j in range(4):
                head = before if j == 0 else pltpu.roll(before, 128 - 32 * j, 1)
                a[c, j, k] = jnp.where(lane < 32, head, pltpu.roll(v[c, j, k], 32, 1))

    quad_step(lambda c, j, k: 8.0 * a[c, j, k], writer(coarse), 2)
    eight_forced_steps(a, b, g)
    blocks = slab_blocks[slab]
    order = single_order()

    @rows_loop
    def _(k):
        for c in range(2):
            made = exchanged([8.0 * a[c, j, k] - coarse[c, j, k] for j in range(4)], (64, 32))
            for i in range(4):
                big[i, c, k] = made[i]

    @rows_loop
    def _(k):
        for c in range(2):
            for i in range(4):
                big[i, c, k] = jnp.where(i < blocks, picked(big[i, c, k], order), 0.0)

    @rows_loop
    def _(k):
        for c in range(2):
            made = [big[i, c, k] for i in range(4)]
            to_left, to_right = pltpu.roll(made[0], 96, 1), pltpu.roll(made[0], 64, 1)
            for i in range(4):
                if i:
                    to_left = jnp.where(lane // 32 == i, pltpu.roll(made[i], (32 * i + 96) % 128, 1), to_left)
                    to_right = jnp.where(lane // 32 == i, pltpu.roll(made[i], (32 * i + 64) % 128, 1), to_right)
            left[c, k] = to_left
            right[c, k] = to_right


def merge_kernel(
    slab_blocks, mine, mine_left, mine_right, mine_init, other, other_left, other_right, other_init, big, init, out
):
    lane = lanes()
    order = single_order()
    slab = lax.axis_index("tm")
    odd = slab % 2

    @rows_loop
    def _(k):
        for slot, centre, lower, upper in (
            (odd, mine, mine_left, mine_right),
            (1 - odd, other, other_left, other_right),
        ):
            for c in range(2):
                low, high = lower[c, k], upper[c, k]
                for i in range(4):
                    u = jnp.where(lane < 32, pltpu.roll(low, 128 - 32 * i, 1) if i else low, centre[i, c, k])
                    u = jnp.where(lane >= 96, pltpu.roll(high, 96 - 32 * i, 1) if i < 3 else high, u)
                    big[4 * slot + i, c, k] = u
        for c in range(2):
            init[c, k] = 8.0 * picked(jnp.where(odd == 1, other_init[c, k], mine_init[c, k]), order)

    sweep_kernel(0)(slab_blocks, init, big, out)


def sweep_kernel(plane):
    def kernel(slab_blocks, state, big, out):
        even = lax.axis_index("tm") // 2 * 2
        before = slab_blocks[even]

        @pl.when(even == 2 * plane)
        def _():
            def turn(n, s):
                slot = jnp.where(n < before, n, n - before + 4)
                p, q = step(s[0], s[1], 2)
                return p + big[slot, 0], q + big[slot, 1]

            p, q = lax.fori_loop(0, before + slab_blocks[even + 1], turn, (state[0], state[1]))
            out[0] = p
            out[1] = q

    kernel.__name__ = "sweep_kernel"
    return kernel


def solution_kernel(slab_blocks, state, big, heads, ends, solved):
    slab = lax.axis_index("tm")
    odd = slab % 2
    before = slab_blocks[slab - odd]
    order = quad_order()

    def turn(i, s):
        solved[jnp.maximum(i, 0), 0] = s[0]
        solved[jnp.maximum(i, 0), 1] = s[1]
        slot = jnp.where(i < 0, i + before, 4 * odd + i)
        p, q = step(s[0], s[1], 2)
        return p + big[slot, 0], q + big[slot, 1]

    p, q = lax.fori_loop(-odd * before, 4, turn, (state[0], state[1]))
    solved[4, 0] = p
    solved[4, 1] = q

    @rows_loop
    def _(k):
        for c in range(2):
            for i in range(5):
                solved[i, c, k] = picked(0.125 * solved[i, c, k], order)

    @rows_loop
    def _(k):
        for c in range(2):
            made = [solved[i, c, k] for i in range(5)]
            first, last = exchanged(made[:4], (64, 32)), exchanged(made[1:], (64, 32))
            for j in range(4):
                heads[c, j, k] = first[j]
                ends[c, j, k] = last[j]


def last_pass_kernel(slab_blocks, heads, ends, g, out, a, b):
    lane = lanes()
    flat = out.reshape(16 * 8 * 4 * 8, 128)
    scale = 1.0 / advection_rate[1]
    of_p = (lane % 32 >= 8) & (lane % 32 < 24)

    def put(t, j, k, p, q):
        u = jnp.where(of_p, p, pltpu.roll(q, 16, 1))
        flat[pl.ds((k // 8) * 256 + t * 32 + j * 8 + k % 8, 8, stride=512), :] = scale * u

    def forced(ref, t):
        def write(j, k, p, q):
            p, q = p + g[t, 0, j, k], q + g[t, 1, j, k]
            ref[0, j, k] = p
            ref[1, j, k] = q
            put(t, j, k, p, q)

        return write

    @in_each
    def _(c, j, k):
        a[c, j, k] = heads[c, j, k]

    @pl.loop(0, 4)
    def _(n):
        quad_step(reader(a), forced(b, 2 * n), 1)
        quad_step(reader(b), forced(a, 2 * n + 1), 1)

    @rows_loop
    def _(k):
        for j in range(4):
            put(7, j, k, ends[0, j, k], ends[1, j, k])


def strips_kernel(slab_blocks, packed, out, made):
    lane = lanes()
    blocks = slab_blocks[lax.axis_index("tm")]
    order = (lane // 64 * 64 + 16 * (lane % 4) + lane % 64 // 4 + 8) % 128

    @pl.loop(0, 8)
    def _(t):
        for n in range(8):
            us = [packed[SNAKE[2 * n + h], t, j] for h in range(2) for j in range(4)]
            for x, u in enumerate(exchanged(us, (64, 32, 16), 8)):
                made[t, n, x] = u

    @pl.loop(0, 8)
    def _(t):
        for n in range(8):
            for i in range(4):
                for c in range(2):
                    u = jnp.where(i < blocks, picked(made[t, n, 2 * i + c], order), 0.0)
                    out[8 * i + t, c, :, 128 * n : 128 * n + 128] = u


def body(init_field, guess, slab_blocks):
    ring = [(k, (k + 1) % 8) for k in range(8)]
    cores = [(k, k ^ 1) for k in range(8)]
    up = [(SNAKE[s], SNAKE[(s + 1) % 16]) for s in range(16)]
    down = [(SNAKE[(s + 1) % 16], SNAKE[s]) for s in range(16)]
    quad_scratch = pltpu.VMEM(QUAD, F32)

    slab = lax.axis_index("tm")
    kind = jnp.sum(jnp.where(jnp.arange(8) == slab, slab_blocks - 1, 0))

    def windows(nb):
        def branch(guess, init_field, slab_blocks):
            number, turns = 2 * nb, 1 if nb == 3 else 4 // nb
            strips = guess.reshape(4, turns, 8 // turns, 2, 8, 1024)
            given = [pl.BlockSpec((nb, turns, 1, 2, 8, 1024), lambda n: (0, 0, n, 0, 0, 0))]
            if nb == 3:
                given.append(pl.BlockSpec((1, 1, 1, 2, 8, 1024), lambda n: (n % 3, 0, 6 + n // 3, 0, 0, 0)))
            pieces = whole(
                windows_kernel(nb),
                shape(16, number, 2, 4, 8, 128),
                (*given, None),
                6,
                [pltpu.VMEM((2, 4, 8, 8, 128), F32)],
                (number,),
            )(slab_blocks, *[strips] * len(given), init_field)
            points = lax.all_to_all(pieces, "space", 0, 0, tiled=True).reshape(16, number, 8, 8, 128)
            if nb == 4:
                return points
            return whole(gather_kernel(nb), shape(16, 8, 8, 8, 128), 1, 3)(slab_blocks, points)

        return branch

    def strips(nb):
        def branch(packed, slab_blocks):
            if nb < 4:
                packed = whole(pack_kernel(nb), shape(16, 2 * nb, 4, 8, 128), 1, 3)(slab_blocks, packed)
            packed = lax.all_to_all(packed, "space", 0, 0, tiled=True)
            if nb < 4:
                packed = whole(spread_kernel(nb), shape(16, 8, 4, 8, 128), 1, 3)(slab_blocks, packed)
            return packed

        return branch

    with jax.named_scope("column_windows"):
        points = lax.switch(kind, [windows(nb) for nb in (1, 2, 3, 4)], guess, init_field, slab_blocks)
        last_two = pl.BlockSpec((16, 2, 8, 8, 128), lambda i: (0, 3, 0, 0, 0))
        tail = whole(tail_kernel, shape(2, *SINGLE), (last_two,), 2, grid=(1,))(slab_blocks, points)
        before = lax.ppermute(tail, "tm", ring)

    with jax.named_scope("fine_and_first_pass"):
        each = pl.BlockSpec((16, 1, 8, 8, 128), lambda t: (0, t, 0, 0, 0))
        fine = whole(
            inner_fine_kernel, shape(6, *QUAD), (each,), 26, (quad_scratch, quad_scratch), grid=(6,)
        )(slab_blocks, points)
        g, v, last, init1 = whole(
            outer_fine_kernel,
            (shape(8, *QUAD), shape(*QUAD), shape(*SINGLE), shape(*SINGLE)),
            (last_two, None, None),
            12,
            (quad_scratch, quad_scratch),
            grid=(1,),
        )(slab_blocks, points, before, fine)
        arrived = lax.ppermute(last, "tm", ring[:-1])

    with jax.named_scope("second_pass"):
        big, left, right = whole(
            second_pass_kernel,
            (shape(4, *SINGLE), shape(*SINGLE), shape(*SINGLE)),
            4,
            4,
            (quad_scratch, quad_scratch, quad_scratch),
        )(slab_blocks, v, arrived, init1, g)

    with jax.named_scope("coarsest_level"):
        upper = lax.ppermute(left, "space", down)
        lower = lax.ppermute(right, "space", up)
        others = [lax.ppermute(x, "tm", cores) for x in (big, lower, upper, init1)]
        full, state, sent = whole(merge_kernel, (shape(8, *SINGLE), shape(*SINGLE), shape(*SINGLE)), 8, 2)(
            slab_blocks, big, lower, upper, init1, *others
        )
        plane = slab // 2
        for turn in range(3):
            if turn:
                sent = whole(sweep_kernel(turn), shape(*SINGLE), 2, 1)(slab_blocks, state, full)
            route = [(2 * turn + core, 2 * turn + 2 + core) for core in range(2)]
            came = lax.ppermute(sent, "tm", route)
            state = jnp.where(plane == turn + 1, came, state)

    with jax.named_scope("last_pass"):
        heads, ends = whole(
            solution_kernel, (shape(*QUAD), shape(*QUAD)), 2, 3, (pltpu.VMEM((5, *SINGLE), F32),)
        )(slab_blocks, state, full)
        packed = whole(last_pass_kernel, shape(16, 8, 4, 8, 128), 3, 6, (quad_scratch, quad_scratch))(
            slab_blocks, heads, ends, g
        )
        packed = lax.switch(kind, [strips(nb) for nb in (1, 2, 3, 4)], packed, slab_blocks)
        return whole(strips_kernel, shape(*guess.shape), 1, 5, (pltpu.VMEM((8, 8, 8, 8, 128), F32),))(
            slab_blocks, packed
        )


def solution(mesh):
    placed = (P(None, "space", None), P("tm", None, "space", None), P())
    return jax.shard_map(
        body, mesh=mesh, in_specs=placed, out_specs=P("tm", None, "space", None), check_vma=False
    )
```

```python
import jax
import jax.numpy as jnp
from jax import lax
from jax.experimental import pallas as pl
from jax.experimental.pallas import tpu as pltpu
from jax.sharding import PartitionSpec as P

diffusion_rate = (0.0035, 0.028, 0.224)
advection_rate = (0.003, 0.024, 0.192)
F32 = jnp.float32

SNAKE = [4 * (s // 4) + (s % 4 if (s // 4) % 2 == 0 else 3 - s % 4) for s in range(16)]
SMEM = pl.BlockSpec(memory_space=pltpu.SMEM)
VMEM = pl.BlockSpec(memory_space=pltpu.VMEM)
SINGLE = (2, 16, 8, 128)
QUAD = (2, 4, 16, 8, 128)


def shape(*dims):
    return jax.ShapeDtypeStruct(dims, F32)


def whole(kernel, outs, inputs, microseconds, scratch=(), grid=()):
    specs = [VMEM] * inputs if isinstance(inputs, int) else [VMEM if x is None else x for x in inputs]
    return pl.pallas_call(
        kernel,
        grid=grid,
        out_shape=outs,
        in_specs=[SMEM] + specs,
        out_specs=jax.tree.map(lambda _: VMEM, outs),
        scratch_shapes=list(scratch),
        compiler_params=pltpu.CompilerParams(vmem_limit_bytes=12 * 1024 * 1024),
        cost_estimate=pl.CostEstimate(
            flops=microseconds * 10**9, bytes_accessed=microseconds * 3 * 10**6, transcendentals=0
        ),
        name=kernel.__name__,
    )


def lanes():
    return lax.broadcasted_iota(jnp.int32, (8, 128), 1)


def picked(u, index):
    return jnp.take_along_axis(u, index, axis=1, mode="promise_in_bounds")


def exchanged(tiles, sizes, first=0):
    tiles, lane = list(tiles), (lanes() + 128 - first) % 128
    apart = len(tiles) // 2
    for size in sizes:
        lower = (lane // size) % 2 == 0
        for a in range(len(tiles)):
            if (a // apart) % 2 == 0:
                x, y = tiles[a], tiles[a + apart]
                tiles[a] = jnp.where(lower, x, pltpu.roll(y, size, 1))
                tiles[a + apart] = jnp.where(lower, pltpu.roll(x, 128 - size, 1), y)
        apart //= 2
    return tiles


def quad_order():
    lane = lanes()
    return 4 * (lane % 32) + lane // 32


def single_order():
    lane = lanes()
    return 32 * (lane % 4) + lane // 4


def step(p, q, level):
    d = diffusion_rate[level]
    sub = lax.broadcasted_iota(jnp.int32, (8, 128), 0)
    wp, ep, sq, nq = d + p, d - p, d + q, d - q

    def one(u):
        after_last = jnp.where(sub == 7, 0.0, pltpu.roll(u[0], 7, 0))
        before_first = jnp.where(sub == 0, 0.0, pltpu.roll(u[15], 1, 0))
        north = jnp.concatenate([u[1:], after_last[None]], 0)
        south = jnp.concatenate([before_first[None], u[:-1]], 0)
        east = pltpu.roll(u, 127, 2)
        west = pltpu.roll(u, 1, 2)
        return (1.0 - 4.0 * d) * u + ep * east + wp * west + nq * north + sq * south

    return one(p), one(q)


def quad_step(read, write, level):
    d = diffusion_rate[level]
    sub = lax.broadcasted_iota(jnp.int32, (8, 128), 0)

    def row(k):
        return [[read(c, j, k) for j in range(4)] for c in range(2)]

    first = row(0)
    south = [[jnp.where(sub == 0, 0.0, pltpu.roll(u, 1, 0)) for u in us] for us in row(15)]
    beyond = [[jnp.where(sub == 7, 0.0, pltpu.roll(u, 7, 0)) for u in us] for us in first]
    here = first
    for k in range(16):
        north = row(k + 1) if k < 15 else beyond
        edge_east = [pltpu.roll(us[0], 127, 1) for us in here]
        edge_west = [pltpu.roll(us[3], 1, 1) for us in here]
        for j in range(4):
            p, q = here[0][j], here[1][j]
            wp, ep, sq, nq = d + p, d - p, d + q, d - q
            made = []
            for c in range(2):
                east = here[c][j + 1] if j < 3 else edge_east[c]
                west = here[c][j - 1] if j > 0 else edge_west[c]
                made.append(
                    ((1.0 - 4.0 * d) * here[c][j] + ep * east)
                    + (wp * west + nq * north[c][j])
                    + sq * south[c][j]
                )
            write(j, k, *made)
        south, here = here, north


def reader(ref, *lead):
    return lambda c, j, k: ref[(*lead, c, j, k)]


def writer(ref, *lead):
    def write(j, k, p, q):
        ref[(*lead, 0, j, k)] = p
        ref[(*lead, 1, j, k)] = q

    return write


def adder(ref, g, t):
    def write(j, k, p, q):
        ref[0, j, k] = p + g[t, 0, j, k]
        ref[1, j, k] = q + g[t, 1, j, k]

    return write


def eight_forced_steps(a, b, g):
    @pl.loop(0, 4)
    def _(n):
        quad_step(reader(a), adder(b, g, 2 * n), 1)
        quad_step(reader(b), adder(a, g, 2 * n + 1), 1)


def rows_loop(body):
    pl.loop(0, 16, unroll=8)(body)


def in_each(body):
    @rows_loop
    def _(k):
        for c in range(2):
            for j in range(4):
                body(c, j, k)


def windows_kernel(nb):
    number = 2 * nb

    def kernel(slab_blocks, guess, init, out, made):
        slab = lax.axis_index("tm")
        blocks = slab_blocks[slab]
        lane = lanes()
        beyond = (lane >= 96, lane < 32)

        @pl.loop(0, 2 * number)
        def _(m):
            n, c = m // 2, m % 2
            last_c_point = (slab == 7) & (n == number - 1)

            def tile(i, at):
                cols = slice(128 * at, 128 * at + 128)
                if nb == 3:
                    block, w = (i, n) if i < 3 else (n % 3, 6 + n // 3)
                    special = last_c_point if i == 3 else None
                else:
                    block, w = i % nb, n + number * (i // nb)
                    special = last_c_point & (block == blocks - 1) if i // nb == 4 // nb - 1 else None
                u = guess[8 * block + w, c, :, cols]
                return u if special is None else jnp.where(special, init[c, :, cols], u)

            for odd in range(2):
                order = (quad_order() + 96 + 64 * odd) % 128
                for i in range(4):
                    for at in range(8):
                        u = jnp.where(beyond[odd], tile(i, (at + 7 + 2 * odd) % 8), tile(i, at))
                        made[odd, i, at] = picked(advection_rate[0] * u, order)
            for odd in range(2):
                for at in range(8):
                    quad = exchanged([made[odd, i, at] for i in range(4)], (64, 32))
                    for j in range(4):
                        out[SNAKE[2 * at + odd], n, c, j] = quad[j]

    kernel.__name__ = "windows_kernel"
    return kernel


def gather_kernel(nb):
    def kernel(slab_blocks, packed, out):
        group = lanes() // 32

        @pl.loop(0, 16 * packed.shape[2], unroll=8)
        def _(m):
            source, x = m // packed.shape[2], m % packed.shape[2]
            us = [packed[source, n, x] for n in range(2 * nb)]
            for n in range(2 * nb):
                out[source, n, x] = us[n]
            for w in range(2):
                if nb == 3:
                    first, second, third = us[3 * w : 3 * w + 3]
                    u = jnp.where(group == 1, pltpu.roll(second, 64, 1), pltpu.roll(first, 32, 1))
                    u = jnp.where(group == 2, pltpu.roll(third, 96, 1), u)
                else:
                    u = pltpu.roll(us[2 * nb - 2 + w], 32 * nb, 1)
                out[source, 6 + w, x] = u

    kernel.__name__ = "gather_kernel"
    return kernel


def spread_kernel(nb):
    number = 2 * nb

    def kernel(slab_blocks, packed, out):
        group = (lanes() + 120) % 128 // 32
        if nb == 3:

            @pl.loop(0, 16 * packed.shape[2], unroll=8)
            def _(m):
                source, x = m // packed.shape[2], m % packed.shape[2]
                us = [packed[source, n, x] for n in range(6)]
                for n in range(6):
                    out[source, n, x] = us[n]
                for w in range(2):
                    first, second, third = us[3 * w : 3 * w + 3]
                    u = jnp.where(group == 1, pltpu.roll(second, 64, 1), pltpu.roll(first, 32, 1))
                    out[source, 6 + w, x] = jnp.where(group == 2, pltpu.roll(third, 96, 1), u)

            return

        @pl.loop(0, 16 * number, unroll=8)
        def _(m):
            source, n = m // number, m % number
            for x in range(packed.shape[2]):
                u = packed[source, n, x]
                for r in range(4 // nb):
                    out[source, n + number * r, x] = pltpu.roll(u, 128 - 32 * nb * r, 1) if r else u

    kernel.__name__ = "spread_kernel"
    return kernel


def pack_kernel(nb):
    number = 2 * nb

    def kernel(slab_blocks, full, out):
        group = (lanes() + 120) % 128 // (32 if nb == 3 else 32 * nb)
        if nb == 3:

            @pl.loop(0, 16 * full.shape[2], unroll=8)
            def _(m):
                target, x = m // full.shape[2], m % full.shape[2]
                for n in range(6):
                    u = pltpu.roll(full[target, 6 + n // 3, x], 96 - 32 * (n % 3), 1)
                    out[target, n, x] = jnp.where(group == 3, u, full[target, n, x])

            return

        @pl.loop(0, 16 * number, unroll=8)
        def _(m):
            target, n = m // number, m % number
            for x in range(full.shape[2]):
                u = full[target, n, x]
                for r in range(1, 4 // nb):
                    u = jnp.where(group == r, pltpu.roll(full[target, n + number * r, x], 32 * nb * r, 1), u)
                out[target, n, x] = u

    kernel.__name__ = "pack_kernel"
    return kernel


def taker(points):
    number = points.shape[1]
    flat = points.reshape(16 * number * 64, 128)

    def taken(n, c, j, k):
        first = (k // 8) * number * 64 + n * 64 + c * 32 + j * 8 + k % 8
        return flat[pl.ds(first, 8, stride=number * 128), :]

    return taken


def tail_kernel(slab_blocks, points, out):
    lane = lanes()
    taken = taker(points)
    shift = 128 - 32 * (slab_blocks[lax.axis_index("tm")] - 1)

    @rows_loop
    def _(k):
        for n in range(2):
            for c in range(2):
                u = pltpu.roll(taken(n, c, 0, k), shift % 128, 1)
                for j in range(1, 4):
                    u = jnp.where(lane // 32 == j, pltpu.roll(taken(n, c, j, k), (shift + 32 * j) % 128, 1), u)
                out[n, c, k] = u


def chain(load, a, b, g, t, middle):
    def six_steps(x, y):
        @pl.loop(0, 3)
        def _(_):
            quad_step(reader(x), writer(y), 0)
            quad_step(reader(y), writer(x), 0)

    def finish(j, k, p, q):
        g[t, 0, j, k] = 8.0 * p - g[t, 0, j, k]
        g[t, 1, j, k] = 8.0 * q - g[t, 1, j, k]

    quad_step(load, writer(b), 0)
    six_steps(b, a)
    quad_step(reader(b), writer(a), 0)
    middle()
    quad_step(lambda c, j, k: 8.0 * a[c, j, k], writer(g, t), 1)
    six_steps(a, b)
    quad_step(reader(a), writer(b), 0)
    quad_step(reader(b), finish, 0)


def inner_fine_kernel(slab_blocks, points, g, a, b):
    taken = taker(points)
    blocks = slab_blocks[lax.axis_index("tm")]

    @pl.loop(0, jnp.minimum(2 * blocks, 6))
    def _(t):
        chain(lambda c, j, k: taken(t, c, j, k), a, b, g, t, lambda: None)

    def spread(target, source, shift):
        @in_each
        def _(c, j, k):
            g[target, c, j, k] = pltpu.roll(g[source, c, j, k], shift, 1)

    @pl.when(blocks == 2)
    def _():
        @pl.loop(0, 2)
        def _(n):
            spread(n + 4, n, 64)

    @pl.when(blocks == 1)
    def _():
        @pl.loop(0, 2)
        def _(n):
            spread(n + 4, n, 64)
            spread(n + 2, n, 96)


def outer_fine_kernel(slab_blocks, points, arrived, inner, g, v, last, init, a, b):
    slab = lax.axis_index("tm")
    lane = lanes()
    taken = taker(points)

    def before(t, c, j, k):
        u = arrived[t, c, k]
        return pltpu.roll(u, 128 - 32 * j, 1) if j else u

    @pl.loop(0, 6)
    def _(t):
        @in_each
        def _(c, j, k):
            g[t + 2, c, j, k] = inner[t, c, j, k]

    def middle(t):
        @pl.when(t == 0)
        def _():
            start = (lane < 32) & (slab == 0)

            @in_each
            def _(c, j, k):
                a[c, j, k] = jnp.where(start, before(1, c, j, k), a[c, j, k])
                v[c, j, k] = 8.0 * a[c, j, k]

    def load(t, c, j, k):
        return jnp.where(lane < 32, before(t, c, j, k), pltpu.roll(taken(t, c, j, k), 32, 1))

    few = slab_blocks[slab] <= 2

    @pl.when(few)
    def _():
        @in_each
        def _(c, j, k):
            a[c, j, k] = load(1, c, j, k)

        @in_each
        def _(c, j, k):
            a[c, j, k] = jnp.where(lane < 64, load(0, c, j, k), pltpu.roll(a[c, j, k], 64, 1))

        chain(reader(a), a, b, g, 0, lambda: middle(0))

        @in_each
        def _(c, j, k):
            g[1, c, j, k] = pltpu.roll(g[0, c, j, k], 64, 1)

    @pl.when(jnp.logical_not(few))
    def _():
        @pl.loop(0, 2)
        def _(t):
            @in_each
            def _(c, j, k):
                a[c, j, k] = load(t, c, j, k)

            chain(reader(a), a, b, g, t, lambda: middle(t))

    eight_forced_steps(v, b, g)
    shift = 128 - 32 * (slab_blocks[slab] - 1)

    @rows_loop
    def _(k):
        for c in range(2):
            x = pltpu.roll(v[c, 0, k], shift % 128, 1)
            for j in range(1, 4):
                x = jnp.where(lane // 32 == j, pltpu.roll(v[c, j, k], (shift + 32 * j) % 128, 1), x)
            init[c, k] = 8.0 * arrived[1, c, k]
            last[c, k] = x


def second_pass_kernel(slab_blocks, v, arrived, init, g, big, left, right, a, b, coarse):
    slab = lax.axis_index("tm")
    lane = lanes()

    @rows_loop
    def _(k):
        for c in range(2):
            before = jnp.where(slab == 0, init[c, k], arrived[c, k])
            for j in range(4):
                head = before if j == 0 else pltpu.roll(before, 128 - 32 * j, 1)
                a[c, j, k] = jnp.where(lane < 32, head, pltpu.roll(v[c, j, k], 32, 1))

    quad_step(lambda c, j, k: 8.0 * a[c, j, k], writer(coarse), 2)
    eight_forced_steps(a, b, g)
    blocks = slab_blocks[slab]
    order = single_order()

    @rows_loop
    def _(k):
        for c in range(2):
            made = exchanged([8.0 * a[c, j, k] - coarse[c, j, k] for j in range(4)], (64, 32))
            for i in range(4):
                big[i, c, k] = made[i]

    @rows_loop
    def _(k):
        for c in range(2):
            for i in range(4):
                big[i, c, k] = jnp.where(i < blocks, picked(big[i, c, k], order), 0.0)

    @rows_loop
    def _(k):
        for c in range(2):
            made = [big[i, c, k] for i in range(4)]
            to_left, to_right = pltpu.roll(made[0], 96, 1), pltpu.roll(made[0], 64, 1)
            for i in range(4):
                if i:
                    to_left = jnp.where(lane // 32 == i, pltpu.roll(made[i], (32 * i + 96) % 128, 1), to_left)
                    to_right = jnp.where(lane // 32 == i, pltpu.roll(made[i], (32 * i + 64) % 128, 1), to_right)
            left[c, k] = to_left
            right[c, k] = to_right


def merge_kernel(
    slab_blocks, mine, mine_left, mine_right, mine_init, other, other_left, other_right, other_init, big, init, out
):
    lane = lanes()
    order = single_order()
    slab = lax.axis_index("tm")
    odd = slab % 2

    @rows_loop
    def _(k):
        for slot, centre, lower, upper in (
            (odd, mine, mine_left, mine_right),
            (1 - odd, other, other_left, other_right),
        ):
            for c in range(2):
                low, high = lower[c, k], upper[c, k]
                for i in range(4):
                    u = jnp.where(lane < 32, pltpu.roll(low, 128 - 32 * i, 1) if i else low, centre[i, c, k])
                    u = jnp.where(lane >= 96, pltpu.roll(high, 96 - 32 * i, 1) if i < 3 else high, u)
                    big[4 * slot + i, c, k] = u
        for c in range(2):
            init[c, k] = 8.0 * picked(jnp.where(odd == 1, other_init[c, k], mine_init[c, k]), order)

    sweep_kernel(0)(slab_blocks, init, big, out)


def sweep_kernel(plane):
    def kernel(slab_blocks, state, big, out):
        even = lax.axis_index("tm") // 2 * 2
        before = slab_blocks[even]

        @pl.when(even == 2 * plane)
        def _():
            def turn(n, s):
                slot = jnp.where(n < before, n, n - before + 4)
                p, q = step(s[0], s[1], 2)
                return p + big[slot, 0], q + big[slot, 1]

            p, q = lax.fori_loop(0, before + slab_blocks[even + 1], turn, (state[0], state[1]))
            out[0] = p
            out[1] = q

    kernel.__name__ = "sweep_kernel"
    return kernel


def solution_kernel(slab_blocks, state, big, heads, ends, solved):
    slab = lax.axis_index("tm")
    odd = slab % 2
    before = slab_blocks[slab - odd]
    order = quad_order()

    def turn(i, s):
        solved[jnp.maximum(i, 0), 0] = s[0]
        solved[jnp.maximum(i, 0), 1] = s[1]
        slot = jnp.where(i < 0, i + before, 4 * odd + i)
        p, q = step(s[0], s[1], 2)
        return p + big[slot, 0], q + big[slot, 1]

    p, q = lax.fori_loop(-odd * before, 4, turn, (state[0], state[1]))
    solved[4, 0] = p
    solved[4, 1] = q

    @rows_loop
    def _(k):
        for c in range(2):
            for i in range(5):
                solved[i, c, k] = picked(0.125 * solved[i, c, k], order)

    @rows_loop
    def _(k):
        for c in range(2):
            made = [solved[i, c, k] for i in range(5)]
            first, last = exchanged(made[:4], (64, 32)), exchanged(made[1:], (64, 32))
            for j in range(4):
                heads[c, j, k] = first[j]
                ends[c, j, k] = last[j]


def last_pass_kernel(slab_blocks, heads, ends, g, out, a, b):
    lane = lanes()
    flat = out.reshape(16 * 8 * 4 * 8, 128)
    scale = 1.0 / advection_rate[1]
    of_p = (lane % 32 >= 8) & (lane % 32 < 24)

    def put(t, ref):
        for j in range(4):
            for k in range(16):
                u = jnp.where(of_p, ref[0, j, k], pltpu.roll(ref[1, j, k], 16, 1))
                flat[pl.ds((k // 8) * 256 + t * 32 + j * 8 + k % 8, 8, stride=512), :] = scale * u

    @in_each
    def _(c, j, k):
        a[c, j, k] = heads[c, j, k]

    @pl.loop(0, 4)
    def _(n):
        quad_step(reader(a), adder(b, g, 2 * n), 1)
        put(2 * n, b)

        @pl.when(n < 3)
        def _():
            quad_step(reader(b), adder(a, g, 2 * n + 1), 1)
            put(2 * n + 1, a)

    put(7, ends)


def strips_kernel(slab_blocks, packed, out, made):
    lane = lanes()
    blocks = slab_blocks[lax.axis_index("tm")]
    order = (lane // 64 * 64 + 16 * (lane % 4) + lane % 64 // 4 + 8) % 128

    def stage(size):
        apart = size // 16
        lower = (lane + 120) % 128 // size % 2 == 0

        @pl.loop(0, 8, unroll=4)
        def _(t):
            for n in range(8):
                for x in range(8):
                    if x // apart % 2 == 0:
                        if size == 64:
                            p, q = packed[SNAKE[2 * n], t, x], packed[SNAKE[2 * n + 1], t, x]
                        else:
                            p, q = made[t, n, x], made[t, n, x + apart]
                        made[t, n, x] = jnp.where(lower, p, pltpu.roll(q, size, 1))
                        made[t, n, x + apart] = jnp.where(lower, pltpu.roll(p, 128 - size, 1), q)

    stage(64)
    stage(32)
    stage(16)

    @pl.loop(0, 8, unroll=4)
    def _(t):
        for n in range(8):
            for i in range(4):
                for c in range(2):
                    u = jnp.where(i < blocks, picked(made[t, n, 2 * i + c], order), 0.0)
                    out[8 * i + t, c, :, 128 * n : 128 * n + 128] = u


def body(init_field, guess, slab_blocks):
    ring = [(k, (k + 1) % 8) for k in range(8)]
    cores = [(k, k ^ 1) for k in range(8)]
    up = [(SNAKE[s], SNAKE[(s + 1) % 16]) for s in range(16)]
    down = [(SNAKE[(s + 1) % 16], SNAKE[s]) for s in range(16)]
    quad_scratch = pltpu.VMEM(QUAD, F32)

    slab = lax.axis_index("tm")
    kind = jnp.sum(jnp.where(jnp.arange(8) == slab, slab_blocks - 1, 0))

    def windows(nb):
        def branch(guess, init_field, slab_blocks):
            number = 2 * nb
            pieces = whole(
                windows_kernel(nb), shape(16, number, 2, 4, 8, 128), 2, 6, [pltpu.VMEM((2, 4, 8, 8, 128), F32)]
            )(slab_blocks, guess, init_field)
            points = lax.all_to_all(pieces, "space", 0, 0, tiled=True).reshape(16, number, 8, 8, 128)
            if nb == 4:
                return points
            return whole(gather_kernel(nb), shape(16, 8, 8, 8, 128), 1, 3)(slab_blocks, points)

        return branch

    def strips(nb):
        def branch(packed, slab_blocks):
            if nb < 4:
                packed = whole(pack_kernel(nb), shape(16, 2 * nb, 4, 8, 128), 1, 3)(slab_blocks, packed)
            packed = lax.all_to_all(packed, "space", 0, 0, tiled=True)
            if nb < 4:
                packed = whole(spread_kernel(nb), shape(16, 8, 4, 8, 128), 1, 3)(slab_blocks, packed)
            return packed

        return branch

    with jax.named_scope("column_windows"):
        points = lax.switch(kind, [windows(nb) for nb in (1, 2, 3, 4)], guess, init_field, slab_blocks)
        last_two = pl.BlockSpec((16, 2, 8, 8, 128), lambda i: (0, 3, 0, 0, 0))
        tail = whole(tail_kernel, shape(2, *SINGLE), (last_two,), 2, grid=(1,))(slab_blocks, points)
        before = lax.ppermute(tail, "tm", ring)

    with jax.named_scope("fine_and_first_pass"):
        fine = whole(inner_fine_kernel, shape(6, *QUAD), 1, 26, (quad_scratch, quad_scratch))(slab_blocks, points)
        g, v, last, init1 = whole(
            outer_fine_kernel,
            (shape(8, *QUAD), shape(*QUAD), shape(*SINGLE), shape(*SINGLE)),
            (last_two, None, None),
            12,
            (quad_scratch, quad_scratch),
            grid=(1,),
        )(slab_blocks, points, before, fine)
        arrived = lax.ppermute(last, "tm", ring[:-1])

    with jax.named_scope("second_pass"):
        big, left, right = whole(
            second_pass_kernel,
            (shape(4, *SINGLE), shape(*SINGLE), shape(*SINGLE)),
            4,
            4,
            (quad_scratch, quad_scratch, quad_scratch),
        )(slab_blocks, v, arrived, init1, g)

    with jax.named_scope("coarsest_level"):
        upper = lax.ppermute(left, "space", down)
        lower = lax.ppermute(right, "space", up)
        others = [lax.ppermute(x, "tm", cores) for x in (big, lower, upper, init1)]
        full, state, sent = whole(merge_kernel, (shape(8, *SINGLE), shape(*SINGLE), shape(*SINGLE)), 8, 2)(
            slab_blocks, big, lower, upper, init1, *others
        )
        plane = slab // 2
        for turn in range(3):
            if turn:
                sent = whole(sweep_kernel(turn), shape(*SINGLE), 2, 1)(slab_blocks, state, full)
            route = [(2 * turn + core, 2 * turn + 2 + core) for core in range(2)]
            came = lax.ppermute(sent, "tm", route)
            state = jnp.where(plane == turn + 1, came, state)

    with jax.named_scope("last_pass"):
        heads, ends = whole(
            solution_kernel, (shape(*QUAD), shape(*QUAD)), 2, 3, (pltpu.VMEM((5, *SINGLE), F32),)
        )(slab_blocks, state, full)
        packed = whole(last_pass_kernel, shape(16, 8, 4, 8, 128), 3, 6, (quad_scratch, quad_scratch))(
            slab_blocks, heads, ends, g
        )
        packed = lax.switch(kind, [strips(nb) for nb in (1, 2, 3, 4)], packed, slab_blocks)
        return whole(strips_kernel, shape(*guess.shape), 1, 5, (pltpu.VMEM((8, 8, 8, 8, 128), F32),))(
            slab_blocks, packed
        )


def solution(mesh):
    placed = (P(None, "space", None), P("tm", None, "space", None), P())
    return jax.shard_map(
        body, mesh=mesh, in_specs=placed, out_specs=P("tm", None, "space", None), check_vma=False
    )
```

```python
import jax
import jax.numpy as jnp
from jax import lax
from jax.experimental import pallas as pl
from jax.experimental.pallas import tpu as pltpu
from jax.sharding import PartitionSpec as P

diffusion_rate = (0.0035, 0.028, 0.224)
advection_rate = (0.003, 0.024, 0.192)
F32 = jnp.float32

SNAKE = [4 * (s // 4) + (s % 4 if (s // 4) % 2 == 0 else 3 - s % 4) for s in range(16)]
SMEM = pl.BlockSpec(memory_space=pltpu.SMEM)
VMEM = pl.BlockSpec(memory_space=pltpu.VMEM)
SINGLE = (2, 16, 8, 128)
QUAD = (2, 4, 16, 8, 128)


def shape(*dims):
    return jax.ShapeDtypeStruct(dims, F32)


def whole(kernel, outs, inputs, microseconds, scratch=(), grid=()):
    specs = [VMEM] * inputs if isinstance(inputs, int) else [VMEM if x is None else x for x in inputs]
    return pl.pallas_call(
        kernel,
        grid=grid,
        out_shape=outs,
        in_specs=[SMEM] + specs,
        out_specs=jax.tree.map(lambda _: VMEM, outs),
        scratch_shapes=list(scratch),
        compiler_params=pltpu.CompilerParams(vmem_limit_bytes=12 * 1024 * 1024),
        cost_estimate=pl.CostEstimate(
            flops=microseconds * 10**9, bytes_accessed=microseconds * 3 * 10**6, transcendentals=0
        ),
        name=kernel.__name__,
    )


def lanes():
    return lax.broadcasted_iota(jnp.int32, (8, 128), 1)


def picked(u, index):
    return jnp.take_along_axis(u, index, axis=1, mode="promise_in_bounds")


def exchanged(tiles, sizes, first=0):
    tiles, lane = list(tiles), (lanes() + 128 - first) % 128
    apart = len(tiles) // 2
    for size in sizes:
        lower = (lane // size) % 2 == 0
        for a in range(len(tiles)):
            if (a // apart) % 2 == 0:
                x, y = tiles[a], tiles[a + apart]
                tiles[a] = jnp.where(lower, x, pltpu.roll(y, size, 1))
                tiles[a + apart] = jnp.where(lower, pltpu.roll(x, 128 - size, 1), y)
        apart //= 2
    return tiles


def quad_order():
    lane = lanes()
    return 4 * (lane % 32) + lane // 32


def single_order():
    lane = lanes()
    return 32 * (lane % 4) + lane // 4


def step(p, q, level):
    d = diffusion_rate[level]
    sub = lax.broadcasted_iota(jnp.int32, (8, 128), 0)
    wp, ep, sq, nq = d + p, d - p, d + q, d - q

    def one(u):
        after_last = jnp.where(sub == 7, 0.0, pltpu.roll(u[0], 7, 0))
        before_first = jnp.where(sub == 0, 0.0, pltpu.roll(u[15], 1, 0))
        north = jnp.concatenate([u[1:], after_last[None]], 0)
        south = jnp.concatenate([before_first[None], u[:-1]], 0)
        east = pltpu.roll(u, 127, 2)
        west = pltpu.roll(u, 1, 2)
        return (1.0 - 4.0 * d) * u + ep * east + wp * west + nq * north + sq * south

    return one(p), one(q)


def quad_step(read, write, level):
    d = diffusion_rate[level]
    sub = lax.broadcasted_iota(jnp.int32, (8, 128), 0)

    def row(k):
        return [[read(c, j, k) for j in range(4)] for c in range(2)]

    first = row(0)
    south = [[jnp.where(sub == 0, 0.0, pltpu.roll(u, 1, 0)) for u in us] for us in row(15)]
    beyond = [[jnp.where(sub == 7, 0.0, pltpu.roll(u, 7, 0)) for u in us] for us in first]
    here = first
    for k in range(16):
        north = row(k + 1) if k < 15 else beyond
        edge_east = [pltpu.roll(us[0], 127, 1) for us in here]
        edge_west = [pltpu.roll(us[3], 1, 1) for us in here]
        for j in range(4):
            p, q = here[0][j], here[1][j]
            wp, ep, sq, nq = d + p, d - p, d + q, d - q
            made = []
            for c in range(2):
                east = here[c][j + 1] if j < 3 else edge_east[c]
                west = here[c][j - 1] if j > 0 else edge_west[c]
                made.append(
                    ((1.0 - 4.0 * d) * here[c][j] + ep * east)
                    + (wp * west + nq * north[c][j])
                    + sq * south[c][j]
                )
            write(j, k, *made)
        south, here = here, north


def reader(ref, *lead):
    return lambda c, j, k: ref[(*lead, c, j, k)]


def writer(ref, *lead):
    def write(j, k, p, q):
        ref[(*lead, 0, j, k)] = p
        ref[(*lead, 1, j, k)] = q

    return write


def adder(ref, g, t):
    def write(j, k, p, q):
        ref[0, j, k] = p + g[t, 0, j, k]
        ref[1, j, k] = q + g[t, 1, j, k]

    return write


def eight_forced_steps(a, b, g):
    @pl.loop(0, 4)
    def _(n):
        quad_step(reader(a), adder(b, g, 2 * n), 1)
        quad_step(reader(b), adder(a, g, 2 * n + 1), 1)


def rows_loop(body):
    pl.loop(0, 16, unroll=8)(body)


def in_each(body):
    @rows_loop
    def _(k):
        for c in range(2):
            for j in range(4):
                body(c, j, k)


def windows_kernel(nb):
    number = 2 * nb

    def kernel(slab_blocks, guess, init, out, made):
        slab = lax.axis_index("tm")
        blocks = slab_blocks[slab]
        lane = lanes()
        beyond = (lane >= 96, lane < 32)

        def tile(i, at, m):
            n, c = m // 2, m % 2
            last_c_point = (slab == 7) & (n == number - 1)
            cols = slice(128 * at, 128 * at + 128)
            if nb == 3:
                block, w = (i, n) if i < 3 else (n % 3, 6 + n // 3)
                special = last_c_point if i == 3 else None
            else:
                block, w = i % nb, n + number * (i // nb)
                special = last_c_point & (block == blocks - 1) if i // nb == 4 // nb - 1 else None
            u = guess[8 * block + w, c, :, cols]
            return u if special is None else jnp.where(special, init[c, :, cols], u)

        for odd in range(2):
            order = (quad_order() + 96 + 64 * odd) % 128

            @pl.loop(0, 2 * number, unroll=4)
            def _(m):
                for i in range(4):
                    for at in range(8):
                        u = jnp.where(beyond[odd], tile(i, (at + 7 + 2 * odd) % 8, m), tile(i, at, m))
                        made[odd, m, i, at] = picked(advection_rate[0] * u, order)

        for size in (64, 32):
            apart = size // 32
            lower = lane // size % 2 == 0

            @pl.loop(0, 2 * number, unroll=4)
            def _(m):
                for odd in range(2):
                    for at in range(8):
                        for x in range(4):
                            if x // apart % 2 == 0:
                                p, q = made[odd, m, x, at], made[odd, m, x + apart, at]
                                p, q = (
                                    jnp.where(lower, p, pltpu.roll(q, size, 1)),
                                    jnp.where(lower, pltpu.roll(p, 128 - size, 1), q),
                                )
                                if size == 64:
                                    made[odd, m, x, at] = p
                                    made[odd, m, x + apart, at] = q
                                else:
                                    out[SNAKE[2 * at + odd], m // 2, m % 2, x] = p
                                    out[SNAKE[2 * at + odd], m // 2, m % 2, x + apart] = q

    kernel.__name__ = "windows_kernel"
    return kernel


def gather_kernel(nb):
    def kernel(slab_blocks, packed, out):
        group = lanes() // 32

        @pl.loop(0, 16 * packed.shape[2], unroll=8)
        def _(m):
            source, x = m // packed.shape[2], m % packed.shape[2]
            us = [packed[source, n, x] for n in range(2 * nb)]
            for n in range(2 * nb):
                out[source, n, x] = us[n]
            for w in range(2):
                if nb == 3:
                    first, second, third = us[3 * w : 3 * w + 3]
                    u = jnp.where(group == 1, pltpu.roll(second, 64, 1), pltpu.roll(first, 32, 1))
                    u = jnp.where(group == 2, pltpu.roll(third, 96, 1), u)
                else:
                    u = pltpu.roll(us[2 * nb - 2 + w], 32 * nb, 1)
                out[source, 6 + w, x] = u

    kernel.__name__ = "gather_kernel"
    return kernel


def spread_kernel(nb):
    number = 2 * nb

    def kernel(slab_blocks, packed, out):
        group = (lanes() + 120) % 128 // 32
        if nb == 3:

            @pl.loop(0, 16 * packed.shape[2], unroll=8)
            def _(m):
                source, x = m // packed.shape[2], m % packed.shape[2]
                us = [packed[source, n, x] for n in range(6)]
                for n in range(6):
                    out[source, n, x] = us[n]
                for w in range(2):
                    first, second, third = us[3 * w : 3 * w + 3]
                    u = jnp.where(group == 1, pltpu.roll(second, 64, 1), pltpu.roll(first, 32, 1))
                    out[source, 6 + w, x] = jnp.where(group == 2, pltpu.roll(third, 96, 1), u)

            return

        @pl.loop(0, 16 * number, unroll=8)
        def _(m):
            source, n = m // number, m % number
            for x in range(packed.shape[2]):
                u = packed[source, n, x]
                for r in range(4 // nb):
                    out[source, n + number * r, x] = pltpu.roll(u, 128 - 32 * nb * r, 1) if r else u

    kernel.__name__ = "spread_kernel"
    return kernel


def pack_kernel(nb):
    number = 2 * nb

    def kernel(slab_blocks, full, out):
        group = (lanes() + 120) % 128 // (32 if nb == 3 else 32 * nb)
        if nb == 3:

            @pl.loop(0, 16 * full.shape[2], unroll=8)
            def _(m):
                target, x = m // full.shape[2], m % full.shape[2]
                for n in range(6):
                    u = pltpu.roll(full[target, 6 + n // 3, x], 96 - 32 * (n % 3), 1)
                    out[target, n, x] = jnp.where(group == 3, u, full[target, n, x])

            return

        @pl.loop(0, 16 * number, unroll=8)
        def _(m):
            target, n = m // number, m % number
            for x in range(full.shape[2]):
                u = full[target, n, x]
                for r in range(1, 4 // nb):
                    u = jnp.where(group == r, pltpu.roll(full[target, n + number * r, x], 32 * nb * r, 1), u)
                out[target, n, x] = u

    kernel.__name__ = "pack_kernel"
    return kernel


def taker(points):
    number = points.shape[1]
    flat = points.reshape(16 * number * 64, 128)

    def taken(n, c, j, k):
        first = (k // 8) * number * 64 + n * 64 + c * 32 + j * 8 + k % 8
        return flat[pl.ds(first, 8, stride=number * 128), :]

    return taken


def tail_kernel(slab_blocks, points, out):
    lane = lanes()
    taken = taker(points)
    shift = 128 - 32 * (slab_blocks[lax.axis_index("tm")] - 1)

    @rows_loop
    def _(k):
        for n in range(2):
            for c in range(2):
                u = pltpu.roll(taken(n, c, 0, k), shift % 128, 1)
                for j in range(1, 4):
                    u = jnp.where(lane // 32 == j, pltpu.roll(taken(n, c, j, k), (shift + 32 * j) % 128, 1), u)
                out[n, c, k] = u


def chain(load, a, b, g, t, middle):
    def six_steps(x, y):
        @pl.loop(0, 3)
        def _(_):
            quad_step(reader(x), writer(y), 0)
            quad_step(reader(y), writer(x), 0)

    def finish(j, k, p, q):
        g[t, 0, j, k] = 8.0 * p - g[t, 0, j, k]
        g[t, 1, j, k] = 8.0 * q - g[t, 1, j, k]

    quad_step(load, writer(b), 0)
    six_steps(b, a)
    quad_step(reader(b), writer(a), 0)
    middle()
    quad_step(lambda c, j, k: 8.0 * a[c, j, k], writer(g, t), 1)
    six_steps(a, b)
    quad_step(reader(a), writer(b), 0)
    quad_step(reader(b), finish, 0)


def inner_fine_kernel(slab_blocks, points, g, a, b):
    taken = taker(points)
    blocks = slab_blocks[lax.axis_index("tm")]

    @pl.loop(0, jnp.minimum(2 * blocks, 6))
    def _(t):
        chain(lambda c, j, k: taken(t, c, j, k), a, b, g, t, lambda: None)

    def spread(target, source, shift):
        @in_each
        def _(c, j, k):
            g[target, c, j, k] = pltpu.roll(g[source, c, j, k], shift, 1)

    @pl.when(blocks == 2)
    def _():
        @pl.loop(0, 2)
        def _(n):
            spread(n + 4, n, 64)

    @pl.when(blocks == 1)
    def _():
        @pl.loop(0, 2)
        def _(n):
            spread(n + 4, n, 64)
            spread(n + 2, n, 96)


def outer_fine_kernel(slab_blocks, points, arrived, inner, g, v, last, init, a, b):
    slab = lax.axis_index("tm")
    lane = lanes()
    taken = taker(points)

    def before(t, c, j, k):
        u = arrived[t, c, k]
        return pltpu.roll(u, 128 - 32 * j, 1) if j else u

    @pl.loop(0, 6)
    def _(t):
        @in_each
        def _(c, j, k):
            g[t + 2, c, j, k] = inner[t, c, j, k]

    def middle(t):
        @pl.when(t == 0)
        def _():
            start = (lane < 32) & (slab == 0)

            @in_each
            def _(c, j, k):
                a[c, j, k] = jnp.where(start, before(1, c, j, k), a[c, j, k])
                v[c, j, k] = 8.0 * a[c, j, k]

    def load(t, c, j, k):
        return jnp.where(lane < 32, before(t, c, j, k), pltpu.roll(taken(t, c, j, k), 32, 1))

    few = slab_blocks[slab] <= 2

    @pl.when(few)
    def _():
        @in_each
        def _(c, j, k):
            a[c, j, k] = load(1, c, j, k)

        @in_each
        def _(c, j, k):
            a[c, j, k] = jnp.where(lane < 64, load(0, c, j, k), pltpu.roll(a[c, j, k], 64, 1))

        chain(reader(a), a, b, g, 0, lambda: middle(0))

        @in_each
        def _(c, j, k):
            g[1, c, j, k] = pltpu.roll(g[0, c, j, k], 64, 1)

    @pl.when(jnp.logical_not(few))
    def _():
        @pl.loop(0, 2)
        def _(t):
            @in_each
            def _(c, j, k):
                a[c, j, k] = load(t, c, j, k)

            chain(reader(a), a, b, g, t, lambda: middle(t))

    eight_forced_steps(v, b, g)
    shift = 128 - 32 * (slab_blocks[slab] - 1)

    @rows_loop
    def _(k):
        for c in range(2):
            x = pltpu.roll(v[c, 0, k], shift % 128, 1)
            for j in range(1, 4):
                x = jnp.where(lane // 32 == j, pltpu.roll(v[c, j, k], (shift + 32 * j) % 128, 1), x)
            init[c, k] = 8.0 * arrived[1, c, k]
            last[c, k] = x


def second_pass_kernel(slab_blocks, v, arrived, init, g, big, left, right, a, b, coarse):
    slab = lax.axis_index("tm")
    lane = lanes()

    @rows_loop
    def _(k):
        for c in range(2):
            before = jnp.where(slab == 0, init[c, k], arrived[c, k])
            for j in range(4):
                head = before if j == 0 else pltpu.roll(before, 128 - 32 * j, 1)
                a[c, j, k] = jnp.where(lane < 32, head, pltpu.roll(v[c, j, k], 32, 1))

    quad_step(lambda c, j, k: 8.0 * a[c, j, k], writer(coarse), 2)
    eight_forced_steps(a, b, g)
    blocks = slab_blocks[slab]
    order = single_order()

    @rows_loop
    def _(k):
        for c in range(2):
            made = exchanged([8.0 * a[c, j, k] - coarse[c, j, k] for j in range(4)], (64, 32))
            for i in range(4):
                big[i, c, k] = made[i]

    @rows_loop
    def _(k):
        for c in range(2):
            for i in range(4):
                big[i, c, k] = jnp.where(i < blocks, picked(big[i, c, k], order), 0.0)

    @rows_loop
    def _(k):
        for c in range(2):
            made = [big[i, c, k] for i in range(4)]
            to_left, to_right = pltpu.roll(made[0], 96, 1), pltpu.roll(made[0], 64, 1)
            for i in range(4):
                if i:
                    to_left = jnp.where(lane // 32 == i, pltpu.roll(made[i], (32 * i + 96) % 128, 1), to_left)
                    to_right = jnp.where(lane // 32 == i, pltpu.roll(made[i], (32 * i + 64) % 128, 1), to_right)
            left[c, k] = to_left
            right[c, k] = to_right


def merge_kernel(
    slab_blocks, mine, mine_left, mine_right, mine_init, other, other_left, other_right, other_init, big, init, out
):
    lane = lanes()
    order = single_order()
    slab = lax.axis_index("tm")
    odd = slab % 2

    @rows_loop
    def _(k):
        for slot, centre, lower, upper in (
            (odd, mine, mine_left, mine_right),
            (1 - odd, other, other_left, other_right),
        ):
            for c in range(2):
                low, high = lower[c, k], upper[c, k]
                for i in range(4):
                    u = jnp.where(lane < 32, pltpu.roll(low, 128 - 32 * i, 1) if i else low, centre[i, c, k])
                    u = jnp.where(lane >= 96, pltpu.roll(high, 96 - 32 * i, 1) if i < 3 else high, u)
                    big[4 * slot + i, c, k] = u
        for c in range(2):
            init[c, k] = 8.0 * picked(jnp.where(odd == 1, other_init[c, k], mine_init[c, k]), order)

    sweep_kernel(0)(slab_blocks, init, big, out)


def sweep_kernel(plane):
    def kernel(slab_blocks, state, big, out):
        even = lax.axis_index("tm") // 2 * 2
        before = slab_blocks[even]

        @pl.when(even == 2 * plane)
        def _():
            def turn(n, s):
                slot = jnp.where(n < before, n, n - before + 4)
                p, q = step(s[0], s[1], 2)
                return p + big[slot, 0], q + big[slot, 1]

            p, q = lax.fori_loop(0, before + slab_blocks[even + 1], turn, (state[0], state[1]))
            out[0] = p
            out[1] = q

    kernel.__name__ = "sweep_kernel"
    return kernel


def solution_kernel(slab_blocks, state, big, heads, ends, solved):
    slab = lax.axis_index("tm")
    odd = slab % 2
    before = slab_blocks[slab - odd]
    order = quad_order()

    def turn(i, s):
        solved[jnp.maximum(i, 0), 0] = s[0]
        solved[jnp.maximum(i, 0), 1] = s[1]
        slot = jnp.where(i < 0, i + before, 4 * odd + i)
        p, q = step(s[0], s[1], 2)
        return p + big[slot, 0], q + big[slot, 1]

    p, q = lax.fori_loop(-odd * before, 4, turn, (state[0], state[1]))
    solved[4, 0] = p
    solved[4, 1] = q

    @rows_loop
    def _(k):
        for c in range(2):
            for i in range(5):
                solved[i, c, k] = picked(0.125 * solved[i, c, k], order)

    @rows_loop
    def _(k):
        for c in range(2):
            made = [solved[i, c, k] for i in range(5)]
            first, last = exchanged(made[:4], (64, 32)), exchanged(made[1:], (64, 32))
            for j in range(4):
                heads[c, j, k] = first[j]
                ends[c, j, k] = last[j]


def last_pass_kernel(slab_blocks, heads, ends, g, out, a, b):
    lane = lanes()
    flat = out.reshape(16 * 8 * 4 * 8, 128)
    scale = 1.0 / advection_rate[1]
    of_p = (lane % 32 >= 8) & (lane % 32 < 24)

    def put(t, ref):
        for j in range(4):
            for k in range(16):
                u = jnp.where(of_p, ref[0, j, k], pltpu.roll(ref[1, j, k], 16, 1))
                flat[pl.ds((k // 8) * 256 + t * 32 + j * 8 + k % 8, 8, stride=512), :] = scale * u

    @in_each
    def _(c, j, k):
        a[c, j, k] = heads[c, j, k]

    @pl.loop(0, 4)
    def _(n):
        quad_step(reader(a), adder(b, g, 2 * n), 1)
        put(2 * n, b)

        @pl.when(n < 3)
        def _():
            quad_step(reader(b), adder(a, g, 2 * n + 1), 1)
            put(2 * n + 1, a)

    put(7, ends)


def strips_kernel(slab_blocks, packed, out, made):
    lane = lanes()
    blocks = slab_blocks[lax.axis_index("tm")]
    order = (lane // 64 * 64 + 16 * (lane % 4) + lane % 64 // 4 + 8) % 128

    def stage(size):
        apart = size // 16
        lower = (lane + 120) % 128 // size % 2 == 0

        @pl.loop(0, 8, unroll=4)
        def _(t):
            for n in range(8):
                for x in range(8):
                    if x // apart % 2 == 0:
                        if size == 64:
                            p, q = packed[SNAKE[2 * n], t, x], packed[SNAKE[2 * n + 1], t, x]
                        else:
                            p, q = made[t, n, x], made[t, n, x + apart]
                        made[t, n, x] = jnp.where(lower, p, pltpu.roll(q, size, 1))
                        made[t, n, x + apart] = jnp.where(lower, pltpu.roll(p, 128 - size, 1), q)

    stage(64)
    stage(32)
    stage(16)

    @pl.loop(0, 8, unroll=4)
    def _(t):
        for n in range(8):
            for i in range(4):
                for c in range(2):
                    u = jnp.where(i < blocks, picked(made[t, n, 2 * i + c], order), 0.0)
                    out[8 * i + t, c, :, 128 * n : 128 * n + 128] = u


def body(init_field, guess, slab_blocks):
    ring = [(k, (k + 1) % 8) for k in range(8)]
    cores = [(k, k ^ 1) for k in range(8)]
    up = [(SNAKE[s], SNAKE[(s + 1) % 16]) for s in range(16)]
    down = [(SNAKE[(s + 1) % 16], SNAKE[s]) for s in range(16)]
    quad_scratch = pltpu.VMEM(QUAD, F32)

    slab = lax.axis_index("tm")
    kind = jnp.sum(jnp.where(jnp.arange(8) == slab, slab_blocks - 1, 0))

    def windows(nb):
        def branch(guess, init_field, slab_blocks):
            number = 2 * nb
            pieces = whole(
                windows_kernel(nb), shape(16, number, 2, 4, 8, 128), 2, 6, [pltpu.VMEM((2, 2 * number, 4, 8, 8, 128), F32)]
            )(slab_blocks, guess, init_field)
            points = lax.all_to_all(pieces, "space", 0, 0, tiled=True).reshape(16, number, 8, 8, 128)
            if nb == 4:
                return points
            return whole(gather_kernel(nb), shape(16, 8, 8, 8, 128), 1, 3)(slab_blocks, points)

        return branch

    def strips(nb):
        def branch(packed, slab_blocks):
            if nb < 4:
                packed = whole(pack_kernel(nb), shape(16, 2 * nb, 4, 8, 128), 1, 3)(slab_blocks, packed)
            packed = lax.all_to_all(packed, "space", 0, 0, tiled=True)
            if nb < 4:
                packed = whole(spread_kernel(nb), shape(16, 8, 4, 8, 128), 1, 3)(slab_blocks, packed)
            return packed

        return branch

    with jax.named_scope("column_windows"):
        points = lax.switch(kind, [windows(nb) for nb in (1, 2, 3, 4)], guess, init_field, slab_blocks)
        last_two = pl.BlockSpec((16, 2, 8, 8, 128), lambda i: (0, 3, 0, 0, 0))
        tail = whole(tail_kernel, shape(2, *SINGLE), (last_two,), 2, grid=(1,))(slab_blocks, points)
        before = lax.ppermute(tail, "tm", ring)

    with jax.named_scope("fine_and_first_pass"):
        fine = whole(inner_fine_kernel, shape(6, *QUAD), 1, 26, (quad_scratch, quad_scratch))(slab_blocks, points)
        g, v, last, init1 = whole(
            outer_fine_kernel,
            (shape(8, *QUAD), shape(*QUAD), shape(*SINGLE), shape(*SINGLE)),
            (last_two, None, None),
            12,
            (quad_scratch, quad_scratch),
            grid=(1,),
        )(slab_blocks, points, before, fine)
        arrived = lax.ppermute(last, "tm", ring[:-1])

    with jax.named_scope("second_pass"):
        big, left, right = whole(
            second_pass_kernel,
            (shape(4, *SINGLE), shape(*SINGLE), shape(*SINGLE)),
            4,
            4,
            (quad_scratch, quad_scratch, quad_scratch),
        )(slab_blocks, v, arrived, init1, g)

    with jax.named_scope("coarsest_level"):
        upper = lax.ppermute(left, "space", down)
        lower = lax.ppermute(right, "space", up)
        others = [lax.ppermute(x, "tm", cores) for x in (big, lower, upper, init1)]
        full, state, sent = whole(merge_kernel, (shape(8, *SINGLE), shape(*SINGLE), shape(*SINGLE)), 8, 2)(
            slab_blocks, big, lower, upper, init1, *others
        )
        plane = slab // 2
        for turn in range(3):
            if turn:
                sent = whole(sweep_kernel(turn), shape(*SINGLE), 2, 1)(slab_blocks, state, full)
            route = [(2 * turn + core, 2 * turn + 2 + core) for core in range(2)]
            came = lax.ppermute(sent, "tm", route)
            state = jnp.where(plane == turn + 1, came, state)

    with jax.named_scope("last_pass"):
        heads, ends = whole(
            solution_kernel, (shape(*QUAD), shape(*QUAD)), 2, 3, (pltpu.VMEM((5, *SINGLE), F32),)
        )(slab_blocks, state, full)
        packed = whole(last_pass_kernel, shape(16, 8, 4, 8, 128), 3, 6, (quad_scratch, quad_scratch))(
            slab_blocks, heads, ends, g
        )
        packed = lax.switch(kind, [strips(nb) for nb in (1, 2, 3, 4)], packed, slab_blocks)
        return whole(strips_kernel, shape(*guess.shape), 1, 5, (pltpu.VMEM((8, 8, 8, 8, 128), F32),))(
            slab_blocks, packed
        )


def solution(mesh):
    placed = (P(None, "space", None), P("tm", None, "space", None), P())
    return jax.shard_map(
        body, mesh=mesh, in_specs=placed, out_specs=P("tm", None, "space", None), check_vma=False
    )
```

```python
import jax
import jax.numpy as jnp
from jax import lax
from jax.experimental import pallas as pl
from jax.experimental.pallas import tpu as pltpu
from jax.sharding import PartitionSpec as P

diffusion_rate = (0.0035, 0.028, 0.224)
advection_rate = (0.003, 0.024, 0.192)
F32 = jnp.float32

SNAKE = [4 * (s // 4) + (s % 4 if (s // 4) % 2 == 0 else 3 - s % 4) for s in range(16)]
SMEM = pl.BlockSpec(memory_space=pltpu.SMEM)
VMEM = pl.BlockSpec(memory_space=pltpu.VMEM)
SINGLE = (2, 16, 8, 128)
QUAD = (2, 4, 16, 8, 128)


def shape(*dims):
    return jax.ShapeDtypeStruct(dims, F32)


def whole(kernel, outs, inputs, microseconds, scratch=(), grid=()):
    specs = [VMEM] * inputs if isinstance(inputs, int) else [VMEM if x is None else x for x in inputs]
    return pl.pallas_call(
        kernel,
        grid=grid,
        out_shape=outs,
        in_specs=[SMEM] + specs,
        out_specs=jax.tree.map(lambda _: VMEM, outs),
        scratch_shapes=list(scratch),
        compiler_params=pltpu.CompilerParams(vmem_limit_bytes=12 * 1024 * 1024),
        cost_estimate=pl.CostEstimate(
            flops=microseconds * 10**9, bytes_accessed=microseconds * 3 * 10**6, transcendentals=0
        ),
        name=kernel.__name__,
    )


def lanes():
    return lax.broadcasted_iota(jnp.int32, (8, 128), 1)


def picked(u, index):
    return jnp.take_along_axis(u, index, axis=1, mode="promise_in_bounds")


def exchanged(tiles, sizes, first=0):
    tiles, lane = list(tiles), (lanes() + 128 - first) % 128
    apart = len(tiles) // 2
    for size in sizes:
        lower = (lane // size) % 2 == 0
        for a in range(len(tiles)):
            if (a // apart) % 2 == 0:
                x, y = tiles[a], tiles[a + apart]
                tiles[a] = jnp.where(lower, x, pltpu.roll(y, size, 1))
                tiles[a + apart] = jnp.where(lower, pltpu.roll(x, 128 - size, 1), y)
        apart //= 2
    return tiles


def quad_order():
    lane = lanes()
    return 4 * (lane % 32) + lane // 32


def single_order():
    lane = lanes()
    return 32 * (lane % 4) + lane // 4


def step(p, q, level):
    d = diffusion_rate[level]
    sub = lax.broadcasted_iota(jnp.int32, (8, 128), 0)
    wp, ep, sq, nq = d + p, d - p, d + q, d - q

    def one(u):
        after_last = jnp.where(sub == 7, 0.0, pltpu.roll(u[0], 7, 0))
        before_first = jnp.where(sub == 0, 0.0, pltpu.roll(u[15], 1, 0))
        north = jnp.concatenate([u[1:], after_last[None]], 0)
        south = jnp.concatenate([before_first[None], u[:-1]], 0)
        east = pltpu.roll(u, 127, 2)
        west = pltpu.roll(u, 1, 2)
        return (1.0 - 4.0 * d) * u + ep * east + wp * west + nq * north + sq * south

    return one(p), one(q)


def quad_step(read, write, level):
    d = diffusion_rate[level]
    sub = lax.broadcasted_iota(jnp.int32, (8, 128), 0)

    def row(k):
        return [[read(c, j, k) for j in range(4)] for c in range(2)]

    first = row(0)
    south = [[jnp.where(sub == 0, 0.0, pltpu.roll(u, 1, 0)) for u in us] for us in row(15)]
    beyond = [[jnp.where(sub == 7, 0.0, pltpu.roll(u, 7, 0)) for u in us] for us in first]
    here = first
    for k in range(16):
        north = row(k + 1) if k < 15 else beyond
        edge_east = [pltpu.roll(us[0], 127, 1) for us in here]
        edge_west = [pltpu.roll(us[3], 1, 1) for us in here]
        for j in range(4):
            p, q = here[0][j], here[1][j]
            wp, ep, sq, nq = d + p, d - p, d + q, d - q
            made = []
            for c in range(2):
                east = here[c][j + 1] if j < 3 else edge_east[c]
                west = here[c][j - 1] if j > 0 else edge_west[c]
                made.append(
                    ((1.0 - 4.0 * d) * here[c][j] + ep * east)
                    + (wp * west + nq * north[c][j])
                    + sq * south[c][j]
                )
            write(j, k, *made)
        south, here = here, north


def reader(ref, *lead):
    return lambda c, j, k: ref[(*lead, c, j, k)]


def writer(ref, *lead):
    def write(j, k, p, q):
        ref[(*lead, 0, j, k)] = p
        ref[(*lead, 1, j, k)] = q

    return write


def adder(ref, g, t):
    def write(j, k, p, q):
        ref[0, j, k] = p + g[t, 0, j, k]
        ref[1, j, k] = q + g[t, 1, j, k]

    return write


def eight_forced_steps(a, b, g):
    @pl.loop(0, 4)
    def _(n):
        quad_step(reader(a), adder(b, g, 2 * n), 1)
        quad_step(reader(b), adder(a, g, 2 * n + 1), 1)


def rows_loop(body):
    pl.loop(0, 16, unroll=8)(body)


def in_each(body):
    @rows_loop
    def _(k):
        for c in range(2):
            for j in range(4):
                body(c, j, k)


def windows_kernel(nb):
    number = 2 * nb

    def kernel(slab_blocks, guess, init, out, made):
        slab = lax.axis_index("tm")
        blocks = slab_blocks[slab]
        lane = lanes()
        beyond = (lane >= 96, lane < 32)

        def tile(i, at, m):
            n, c = m // 2, m % 2
            last_c_point = (slab == 7) & (n == number - 1)
            cols = slice(128 * at, 128 * at + 128)
            if nb == 3:
                block, w = (i, n) if i < 3 else (n % 3, 6 + n // 3)
                special = last_c_point if i == 3 else None
            else:
                block, w = i % nb, n + number * (i // nb)
                special = last_c_point & (block == blocks - 1) if i // nb == 4 // nb - 1 else None
            u = guess[8 * block + w, c, :, cols]
            return u if special is None else jnp.where(special, init[c, :, cols], u)

        for odd in range(2):
            order = (quad_order() + 96 + 64 * odd) % 128

            @pl.loop(0, 2 * number, unroll=4)
            def _(m):
                for i in range(4):
                    for at in range(8):
                        u = jnp.where(beyond[odd], tile(i, (at + 7 + 2 * odd) % 8, m), tile(i, at, m))
                        made[odd, m, i, at] = picked(advection_rate[0] * u, order)

        for size in (64, 32):
            apart = size // 32
            lower = lane // size % 2 == 0

            @pl.loop(0, 2 * number, unroll=4)
            def _(m):
                for odd in range(2):
                    for at in range(8):
                        for x in range(4):
                            if x // apart % 2 == 0:
                                p, q = made[odd, m, x, at], made[odd, m, x + apart, at]
                                p, q = (
                                    jnp.where(lower, p, pltpu.roll(q, size, 1)),
                                    jnp.where(lower, pltpu.roll(p, 128 - size, 1), q),
                                )
                                if size == 64:
                                    made[odd, m, x, at] = p
                                    made[odd, m, x + apart, at] = q
                                else:
                                    out[SNAKE[2 * at + odd], m // 2, m % 2, x] = p
                                    out[SNAKE[2 * at + odd], m // 2, m % 2, x + apart] = q

    kernel.__name__ = "windows_kernel"
    return kernel


def gather_kernel(nb):
    def kernel(slab_blocks, packed, out):
        group = lanes() // 32

        @pl.loop(0, 16 * packed.shape[2], unroll=16)
        def _(m):
            source, x = m // packed.shape[2], m % packed.shape[2]
            us = [packed[source, n, x] for n in range(2 * nb)]
            for n in range(2 * nb):
                out[source, n, x] = us[n]
            for w in range(2):
                if nb == 3:
                    first, second, third = us[3 * w : 3 * w + 3]
                    u = jnp.where(group == 1, pltpu.roll(second, 64, 1), pltpu.roll(first, 32, 1))
                    u = jnp.where(group == 2, pltpu.roll(third, 96, 1), u)
                else:
                    u = pltpu.roll(us[2 * nb - 2 + w], 32 * nb, 1)
                out[source, 6 + w, x] = u

    kernel.__name__ = "gather_kernel"
    return kernel


def spread_kernel(nb):
    number = 2 * nb

    def kernel(slab_blocks, packed, out):
        group = (lanes() + 120) % 128 // 32
        if nb == 3:

            @pl.loop(0, 16 * packed.shape[2], unroll=16)
            def _(m):
                source, x = m // packed.shape[2], m % packed.shape[2]
                us = [packed[source, n, x] for n in range(6)]
                for n in range(6):
                    out[source, n, x] = us[n]
                for w in range(2):
                    first, second, third = us[3 * w : 3 * w + 3]
                    u = jnp.where(group == 1, pltpu.roll(second, 64, 1), pltpu.roll(first, 32, 1))
                    out[source, 6 + w, x] = jnp.where(group == 2, pltpu.roll(third, 96, 1), u)

            return

        @pl.loop(0, 16 * number, unroll=32)
        def _(m):
            source, n = m // number, m % number
            for x in range(packed.shape[2]):
                u = packed[source, n, x]
                for r in range(4 // nb):
                    out[source, n + number * r, x] = pltpu.roll(u, 128 - 32 * nb * r, 1) if r else u

    kernel.__name__ = "spread_kernel"
    return kernel


def pack_kernel(nb):
    number = 2 * nb

    def kernel(slab_blocks, full, out):
        group = (lanes() + 120) % 128 // (32 if nb == 3 else 32 * nb)
        if nb == 3:

            @pl.loop(0, 16 * full.shape[2], unroll=16)
            def _(m):
                target, x = m // full.shape[2], m % full.shape[2]
                for n in range(6):
                    u = pltpu.roll(full[target, 6 + n // 3, x], 96 - 32 * (n % 3), 1)
                    out[target, n, x] = jnp.where(group == 3, u, full[target, n, x])

            return

        @pl.loop(0, 16 * number, unroll=32)
        def _(m):
            target, n = m // number, m % number
            for x in range(full.shape[2]):
                u = full[target, n, x]
                for r in range(1, 4 // nb):
                    u = jnp.where(group == r, pltpu.roll(full[target, n + number * r, x], 32 * nb * r, 1), u)
                out[target, n, x] = u

    kernel.__name__ = "pack_kernel"
    return kernel


def taker(points):
    number = points.shape[1]
    flat = points.reshape(16 * number * 64, 128)

    def taken(n, c, j, k):
        first = (k // 8) * number * 64 + n * 64 + c * 32 + j * 8 + k % 8
        return flat[pl.ds(first, 8, stride=number * 128), :]

    return taken


def tail_kernel(slab_blocks, points, out):
    lane = lanes()
    taken = taker(points)
    shift = 128 - 32 * (slab_blocks[lax.axis_index("tm")] - 1)

    @rows_loop
    def _(k):
        for n in range(2):
            for c in range(2):
                u = pltpu.roll(taken(n, c, 0, k), shift % 128, 1)
                for j in range(1, 4):
                    u = jnp.where(lane // 32 == j, pltpu.roll(taken(n, c, j, k), (shift + 32 * j) % 128, 1), u)
                out[n, c, k] = u


def chain(load, a, b, g, t, middle):
    def six_steps(x, y):
        @pl.loop(0, 3)
        def _(_):
            quad_step(reader(x), writer(y), 0)
            quad_step(reader(y), writer(x), 0)

    def finish(j, k, p, q):
        g[t, 0, j, k] = 8.0 * p - g[t, 0, j, k]
        g[t, 1, j, k] = 8.0 * q - g[t, 1, j, k]

    quad_step(load, writer(b), 0)
    six_steps(b, a)
    quad_step(reader(b), writer(a), 0)
    middle()
    quad_step(lambda c, j, k: 8.0 * a[c, j, k], writer(g, t), 1)
    six_steps(a, b)
    quad_step(reader(a), writer(b), 0)
    quad_step(reader(b), finish, 0)


def inner_fine_kernel(slab_blocks, points, g, a, b):
    taken = taker(points)
    blocks = slab_blocks[lax.axis_index("tm")]

    @pl.loop(0, jnp.minimum(2 * blocks, 6))
    def _(t):
        chain(lambda c, j, k: taken(t, c, j, k), a, b, g, t, lambda: None)

    def spread(target, source, shift):
        @in_each
        def _(c, j, k):
            g[target, c, j, k] = pltpu.roll(g[source, c, j, k], shift, 1)

    @pl.when(blocks == 2)
    def _():
        @pl.loop(0, 2)
        def _(n):
            spread(n + 4, n, 64)

    @pl.when(blocks == 1)
    def _():
        @pl.loop(0, 2)
        def _(n):
            spread(n + 4, n, 64)
            spread(n + 2, n, 96)


def outer_fine_kernel(slab_blocks, points, arrived, inner, g, v, last, init, a, b):
    slab = lax.axis_index("tm")
    lane = lanes()
    taken = taker(points)

    def before(t, c, j, k):
        u = arrived[t, c, k]
        return pltpu.roll(u, 128 - 32 * j, 1) if j else u

    @pl.loop(0, 6)
    def _(t):
        @in_each
        def _(c, j, k):
            g[t + 2, c, j, k] = inner[t, c, j, k]

    def middle(t):
        @pl.when(t == 0)
        def _():
            start = (lane < 32) & (slab == 0)

            @in_each
            def _(c, j, k):
                a[c, j, k] = jnp.where(start, before(1, c, j, k), a[c, j, k])
                v[c, j, k] = 8.0 * a[c, j, k]

    def load(t, c, j, k):
        return jnp.where(lane < 32, before(t, c, j, k), pltpu.roll(taken(t, c, j, k), 32, 1))

    few = slab_blocks[slab] <= 2

    @pl.when(few)
    def _():
        @in_each
        def _(c, j, k):
            a[c, j, k] = load(1, c, j, k)

        @in_each
        def _(c, j, k):
            a[c, j, k] = jnp.where(lane < 64, load(0, c, j, k), pltpu.roll(a[c, j, k], 64, 1))

        chain(reader(a), a, b, g, 0, lambda: middle(0))

        @in_each
        def _(c, j, k):
            g[1, c, j, k] = pltpu.roll(g[0, c, j, k], 64, 1)

    @pl.when(jnp.logical_not(few))
    def _():
        @pl.loop(0, 2)
        def _(t):
            @in_each
            def _(c, j, k):
                a[c, j, k] = load(t, c, j, k)

            chain(reader(a), a, b, g, t, lambda: middle(t))

    eight_forced_steps(v, b, g)
    shift = 128 - 32 * (slab_blocks[slab] - 1)

    @rows_loop
    def _(k):
        for c in range(2):
            x = pltpu.roll(v[c, 0, k], shift % 128, 1)
            for j in range(1, 4):
                x = jnp.where(lane // 32 == j, pltpu.roll(v[c, j, k], (shift + 32 * j) % 128, 1), x)
            init[c, k] = 8.0 * arrived[1, c, k]
            last[c, k] = x


def second_pass_kernel(slab_blocks, v, arrived, init, g, big, left, right, a, b, coarse):
    slab = lax.axis_index("tm")
    lane = lanes()

    @rows_loop
    def _(k):
        for c in range(2):
            before = jnp.where(slab == 0, init[c, k], arrived[c, k])
            for j in range(4):
                head = before if j == 0 else pltpu.roll(before, 128 - 32 * j, 1)
                a[c, j, k] = jnp.where(lane < 32, head, pltpu.roll(v[c, j, k], 32, 1))

    quad_step(lambda c, j, k: 8.0 * a[c, j, k], writer(coarse), 2)
    eight_forced_steps(a, b, g)
    blocks = slab_blocks[slab]
    order = single_order()

    @rows_loop
    def _(k):
        for c in range(2):
            made = exchanged([8.0 * a[c, j, k] - coarse[c, j, k] for j in range(4)], (64, 32))
            for i in range(4):
                big[i, c, k] = made[i]

    @rows_loop
    def _(k):
        for c in range(2):
            for i in range(4):
                big[i, c, k] = jnp.where(i < blocks, picked(big[i, c, k], order), 0.0)

    @rows_loop
    def _(k):
        for c in range(2):
            made = [big[i, c, k] for i in range(4)]
            to_left, to_right = pltpu.roll(made[0], 96, 1), pltpu.roll(made[0], 64, 1)
            for i in range(4):
                if i:
                    to_left = jnp.where(lane // 32 == i, pltpu.roll(made[i], (32 * i + 96) % 128, 1), to_left)
                    to_right = jnp.where(lane // 32 == i, pltpu.roll(made[i], (32 * i + 64) % 128, 1), to_right)
            left[c, k] = to_left
            right[c, k] = to_right


def merge_kernel(
    slab_blocks, mine, mine_left, mine_right, mine_init, other, other_left, other_right, other_init, big, init, out
):
    lane = lanes()
    order = single_order()
    slab = lax.axis_index("tm")
    odd = slab % 2

    @rows_loop
    def _(k):
        for slot, centre, lower, upper in (
            (odd, mine, mine_left, mine_right),
            (1 - odd, other, other_left, other_right),
        ):
            for c in range(2):
                low, high = lower[c, k], upper[c, k]
                for i in range(4):
                    u = jnp.where(lane < 32, pltpu.roll(low, 128 - 32 * i, 1) if i else low, centre[i, c, k])
                    u = jnp.where(lane >= 96, pltpu.roll(high, 96 - 32 * i, 1) if i < 3 else high, u)
                    big[4 * slot + i, c, k] = u
        for c in range(2):
            init[c, k] = 8.0 * picked(jnp.where(odd == 1, other_init[c, k], mine_init[c, k]), order)

    sweep_kernel(0)(slab_blocks, init, big, out)


def sweep_kernel(plane):
    def kernel(slab_blocks, state, big, out):
        even = lax.axis_index("tm") // 2 * 2
        before = slab_blocks[even]

        @pl.when(even == 2 * plane)
        def _():
            def turn(n, s):
                slot = jnp.where(n < before, n, n - before + 4)
                p, q = step(s[0], s[1], 2)
                return p + big[slot, 0], q + big[slot, 1]

            p, q = lax.fori_loop(0, before + slab_blocks[even + 1], turn, (state[0], state[1]))
            out[0] = p
            out[1] = q

    kernel.__name__ = "sweep_kernel"
    return kernel


def solution_kernel(slab_blocks, state, big, heads, ends, solved):
    slab = lax.axis_index("tm")
    odd = slab % 2
    before = slab_blocks[slab - odd]
    order = quad_order()

    def turn(i, s):
        solved[jnp.maximum(i, 0), 0] = s[0]
        solved[jnp.maximum(i, 0), 1] = s[1]
        slot = jnp.where(i < 0, i + before, 4 * odd + i)
        p, q = step(s[0], s[1], 2)
        return p + big[slot, 0], q + big[slot, 1]

    p, q = lax.fori_loop(-odd * before, 4, turn, (state[0], state[1]))
    solved[4, 0] = p
    solved[4, 1] = q

    @rows_loop
    def _(k):
        for c in range(2):
            for i in range(5):
                solved[i, c, k] = picked(0.125 * solved[i, c, k], order)

    @rows_loop
    def _(k):
        for c in range(2):
            made = [solved[i, c, k] for i in range(5)]
            first, last = exchanged(made[:4], (64, 32)), exchanged(made[1:], (64, 32))
            for j in range(4):
                heads[c, j, k] = first[j]
                ends[c, j, k] = last[j]


def last_pass_kernel(slab_blocks, heads, ends, g, out, a, b):
    lane = lanes()
    flat = out.reshape(16 * 8 * 4 * 8, 128)
    scale = 1.0 / advection_rate[1]
    of_p = (lane % 32 >= 8) & (lane % 32 < 24)

    def put(t, ref):
        for j in range(4):
            for k in range(16):
                u = jnp.where(of_p, ref[0, j, k], pltpu.roll(ref[1, j, k], 16, 1))
                flat[pl.ds((k // 8) * 256 + t * 32 + j * 8 + k % 8, 8, stride=512), :] = scale * u

    @in_each
    def _(c, j, k):
        a[c, j, k] = heads[c, j, k]

    @pl.loop(0, 4)
    def _(n):
        quad_step(reader(a), adder(b, g, 2 * n), 1)
        put(2 * n, b)

        @pl.when(n < 3)
        def _():
            quad_step(reader(b), adder(a, g, 2 * n + 1), 1)
            put(2 * n + 1, a)

    put(7, ends)


def strips_kernel(slab_blocks, packed, out, made):
    lane = lanes()
    blocks = slab_blocks[lax.axis_index("tm")]
    order = (lane // 64 * 64 + 16 * (lane % 4) + lane % 64 // 4 + 8) % 128

    def stage(size):
        apart = size // 16
        lower = (lane + 120) % 128 // size % 2 == 0

        @pl.loop(0, 8, unroll=4)
        def _(t):
            for n in range(8):
                for x in range(8):
                    if x // apart % 2 == 0:
                        if size == 64:
                            p, q = packed[SNAKE[2 * n], t, x], packed[SNAKE[2 * n + 1], t, x]
                        else:
                            p, q = made[t, n, x], made[t, n, x + apart]
                        made[t, n, x] = jnp.where(lower, p, pltpu.roll(q, size, 1))
                        made[t, n, x + apart] = jnp.where(lower, pltpu.roll(p, 128 - size, 1), q)

    stage(64)
    stage(32)
    stage(16)

    @pl.loop(0, 8, unroll=4)
    def _(t):
        for n in range(8):
            for i in range(4):
                for c in range(2):
                    u = jnp.where(i < blocks, picked(made[t, n, 2 * i + c], order), 0.0)
                    out[8 * i + t, c, :, 128 * n : 128 * n + 128] = u


def body(init_field, guess, slab_blocks):
    ring = [(k, (k + 1) % 8) for k in range(8)]
    cores = [(k, k ^ 1) for k in range(8)]
    up = [(SNAKE[s], SNAKE[(s + 1) % 16]) for s in range(16)]
    down = [(SNAKE[(s + 1) % 16], SNAKE[s]) for s in range(16)]
    quad_scratch = pltpu.VMEM(QUAD, F32)

    slab = lax.axis_index("tm")
    kind = jnp.sum(jnp.where(jnp.arange(8) == slab, slab_blocks - 1, 0))

    def windows(nb):
        def branch(guess, init_field, slab_blocks):
            number = 2 * nb
            pieces = whole(
                windows_kernel(nb), shape(16, number, 2, 4, 8, 128), 2, 6, [pltpu.VMEM((2, 2 * number, 4, 8, 8, 128), F32)]
            )(slab_blocks, guess, init_field)
            points = lax.all_to_all(pieces, "space", 0, 0, tiled=True).reshape(16, number, 8, 8, 128)
            if nb == 4:
                return points
            return whole(gather_kernel(nb), shape(16, 8, 8, 8, 128), 1, 3)(slab_blocks, points)

        return branch

    def strips(nb):
        def branch(packed, slab_blocks):
            if nb < 4:
                packed = whole(pack_kernel(nb), shape(16, 2 * nb, 4, 8, 128), 1, 3)(slab_blocks, packed)
            packed = lax.all_to_all(packed, "space", 0, 0, tiled=True)
            if nb < 4:
                packed = whole(spread_kernel(nb), shape(16, 8, 4, 8, 128), 1, 3)(slab_blocks, packed)
            return packed

        return branch

    with jax.named_scope("column_windows"):
        points = lax.switch(kind, [windows(nb) for nb in (1, 2, 3, 4)], guess, init_field, slab_blocks)
        last_two = pl.BlockSpec((16, 2, 8, 8, 128), lambda i: (0, 3, 0, 0, 0))
        tail = whole(tail_kernel, shape(2, *SINGLE), (last_two,), 2, grid=(1,))(slab_blocks, points)
        before = lax.ppermute(tail, "tm", ring)

    with jax.named_scope("fine_and_first_pass"):
        fine = whole(inner_fine_kernel, shape(6, *QUAD), 1, 26, (quad_scratch, quad_scratch))(slab_blocks, points)
        g, v, last, init1 = whole(
            outer_fine_kernel,
            (shape(8, *QUAD), shape(*QUAD), shape(*SINGLE), shape(*SINGLE)),
            (last_two, None, None),
            12,
            (quad_scratch, quad_scratch),
            grid=(1,),
        )(slab_blocks, points, before, fine)
        arrived = lax.ppermute(last, "tm", ring[:-1])

    with jax.named_scope("second_pass"):
        big, left, right = whole(
            second_pass_kernel,
            (shape(4, *SINGLE), shape(*SINGLE), shape(*SINGLE)),
            4,
            4,
            (quad_scratch, quad_scratch, quad_scratch),
        )(slab_blocks, v, arrived, init1, g)

    with jax.named_scope("coarsest_level"):
        upper = lax.ppermute(left, "space", down)
        lower = lax.ppermute(right, "space", up)
        others = [lax.ppermute(x, "tm", cores) for x in (big, lower, upper, init1)]
        full, state, sent = whole(merge_kernel, (shape(8, *SINGLE), shape(*SINGLE), shape(*SINGLE)), 8, 2)(
            slab_blocks, big, lower, upper, init1, *others
        )
        plane = slab // 2
        for turn in range(3):
            if turn:
                sent = whole(sweep_kernel(turn), shape(*SINGLE), 2, 1)(slab_blocks, state, full)
            route = [(2 * turn + core, 2 * turn + 2 + core) for core in range(2)]
            came = lax.ppermute(sent, "tm", route)
            state = jnp.where(plane == turn + 1, came, state)

    with jax.named_scope("last_pass"):
        heads, ends = whole(
            solution_kernel, (shape(*QUAD), shape(*QUAD)), 2, 3, (pltpu.VMEM((5, *SINGLE), F32),)
        )(slab_blocks, state, full)
        packed = whole(last_pass_kernel, shape(16, 8, 4, 8, 128), 3, 6, (quad_scratch, quad_scratch))(
            slab_blocks, heads, ends, g
        )
        packed = lax.switch(kind, [strips(nb) for nb in (1, 2, 3, 4)], packed, slab_blocks)
        return whole(strips_kernel, shape(*guess.shape), 1, 5, (pltpu.VMEM((8, 8, 8, 8, 128), F32),))(
            slab_blocks, packed
        )


def solution(mesh):
    placed = (P(None, "space", None), P("tm", None, "space", None), P())
    return jax.shard_map(
        body, mesh=mesh, in_specs=placed, out_specs=P("tm", None, "space", None), check_vma=False
    )
```
